256 devices in a mesh: gx: 32 (over y_hi, z, core), gy: 8 (over y_lo, x).
Axes of the slice: x: 4, y: 4 (y_hi: 2, y_lo: 2; y = y_hi * 2 + y_lo), z: 8, core: 2. Of those that a mesh axis runs over, the one named last changes fastest.
Arguments:
- positions: float32 [3, 524288], P(None, ('gx', 'gy')), may hold values from 0 to 6
- features: bfloat16 [64, 524288], P(None, ('gx', 'gy')), may hold values from -6 to 6
- halo_lists: int32 [2, 393216], P(None, ('gx', 'gy')), may hold values from 0 to 2047
- local_pairs: int32 [4, 1572864], P(None, ('gx', 'gy')), may hold values from 0 to 2047, as said below
- cross_x: int32 [4, 524288], P(None, ('gx', 'gy')), may hold values from 0 to 2047, as said below
- cross_y: int32 [4, 524288], P(None, ('gx', 'gy')), may hold values from 0 to 2047, as said below
- pair_counts: int32 [256, 3], P(('gx', 'gy')), may hold values from 256 to 6144, as said below
- w_rbf: bfloat16 [8, 256], replicated, may hold values from -2 to 2
- w_src: bfloat16 [64, 256], replicated, may hold values from -0.75 to 0.75
- w_dst: bfloat16 [64, 256], replicated, may hold values from -0.75 to 0.75
- species_src: bfloat16 [4, 256], replicated, may hold values from -3 to 3
- species_dst: bfloat16 [4, 256], replicated, may hold values from -3 to 3
- w_hidden: bfloat16 [256, 256], replicated, may hold values from -0.375 to 0.375
- w_latent: bfloat16 [256, 64], replicated, may hold values from -0.375 to 0.375
- w_energy: float32 [64], replicated, may hold values from -0.75 to 0.75
Outputs:
- energy: float32 [1], replicated
- forces: float32 [3, 524288], P(None, ('gx', 'gy'))
- feature_grads: float32 [64, 524288], P(None, ('gx', 'gy'))
The draws below stay inside these ranges and needn't reach their ends.
Inputs may be any that keep to these rules, and one draw needn't show every extreme that they name: `local_pairs`: rows 0 and 1 are different atoms of the block, below 2048; rows 2 and 3 are species below 4. `cross_x`: row 0 an atom below 2048, row 1 a slot below 1536, rows 2 and 3 species below 4. `cross_y`: row 0 an atom below 2048, row 1 a slot below 1536, rows 2 and 3 species below 4. `pair_counts`: column 0 counts live slots of local_pairs (at most 6144), columns 1 and 2 those of cross_x and cross_y (at most 2048); live slots come first; some device is full in each column.
All inputs are finite; a program needn't handle non-finite values.
Results may differ from the reference program's by a relative error of at most 0.0095.
Values may be sent and summed in bfloat16 or wider, within the bound.
A program may use at most 64 MiB of HBM per device.

```python
import jax
import jax.numpy as jnp
from jax import lax

NRBF = 8
FEAT = 64
HID = 256
NSPEC = 4
BLOCK = 512
A_DEV = 2048
E_LOC = 6144
E_X = 2048
HALO = 1536
ATOMS = 524288
N_GX = 32
N_GY = 8


def draw_local_pairs(key, part):
    keys = jax.random.split(jax.random.fold_in(key, 3), 4)
    total = E_LOC * N_GX * N_GY
    source = jax.random.randint(keys[0], (total,), 0, A_DEV)
    source = source.at[0].set(A_DEV - 1)
    target = (source + jax.random.randint(keys[1], (total,), 1, A_DEV)) % A_DEV
    kind_one = jax.random.randint(keys[2], (total,), 0, NSPEC)
    kind_two = jax.random.randint(keys[3], (total,), 0, NSPEC)
    return jnp.stack([source, target, kind_one, kind_two]).astype(jnp.int32)


def cross_lists(key, salt):
    keys = jax.random.split(jax.random.fold_in(key, salt), 4)
    total = E_X * N_GX * N_GY
    source = jax.random.randint(keys[0], (total,), 0, A_DEV)
    source = source.at[0].set(A_DEV - 1)
    slots = jax.random.randint(keys[1], (total,), 0, HALO)
    kind_one = jax.random.randint(keys[2], (total,), 0, NSPEC)
    kind_two = jax.random.randint(keys[3], (total,), 0, NSPEC)
    return jnp.stack([source, slots, kind_one, kind_two]).astype(jnp.int32)


def draw_cross_x(key, part):
    return cross_lists(key, 5)


def draw_cross_y(key, part):
    return cross_lists(key, 7)


def draw_pair_counts(key, part):
    keys = jax.random.split(jax.random.fold_in(key, 9), 2)
    devices = N_GX * N_GY
    limits = jnp.array([E_LOC, E_X, E_X], jnp.int32)
    levels = jax.random.randint(keys[0], (devices, 3), 0, 4).astype(jnp.int32)
    counts = jnp.right_shift(limits[None, :], levels)
    fullest = jax.random.randint(keys[1], (3,), 0, devices)
    ranks = jnp.arange(devices, dtype=jnp.int32)[:, None]
    return jnp.where(ranks == fullest[None, :], limits[None, :], counts).astype(jnp.int32)


def set_ends(entries, rng, smallest, largest):
    dims = entries.shape
    spot = [jax.random.randint(jax.random.fold_in(rng, axis), (), 0, dims[axis]) for axis in range(len(dims))]
    entries = entries.at[tuple(spot)].set(smallest)
    longest = dims.index(max(dims))
    spot[longest] = (spot[longest] + 1) % dims[longest]
    return entries.at[tuple(spot)].set(largest)


def steps_of(key, extent, cuts, smallest, top_value):
    gain, own = 1.0, jax.random.fold_in(key, 6)
    for dim, blocks in cuts:
        steps = jnp.exp(jax.random.uniform(jax.random.fold_in(own, dim), (blocks,), jnp.float32, smallest / len(cuts), top_value / len(cuts)))
        gain = gain * jnp.repeat(steps, extent[dim] // blocks).reshape([-1 if axis == dim else 1 for axis in range(len(extent))])
    return gain


def scatter_about(own_key, dims, deviation, bound, cuts=(), kind=jnp.bfloat16):
    values = deviation * jax.random.normal(own_key, dims, jnp.float32)
    if cuts:
        values = values * steps_of(own_key, dims, cuts, -0.22, 0.18)
    return jnp.clip(values, -bound, bound).astype(kind)


def setup_inputs(seed: int = 0) -> dict:
    seeds = jax.random.split(jax.random.key(seed), 16)
    positions = jnp.clip(6.0 * jax.random.uniform(seeds[0], (3, ATOMS), jnp.float32) ** steps_of(seeds[0], (3, ATOMS), ((1, 256),), -0.2, 0.2), 0.0, 6.0)
    features = scatter_about(seeds[1], (FEAT, ATOMS), 1.0, 6.0, ((1, 256),))
    halo_lists = set_ends(jax.random.randint(seeds[2], (2, HALO * N_GX * N_GY), 0, A_DEV), jax.random.fold_in(seeds[2], 1), 0, A_DEV - 1).astype(jnp.int32)
    local_pairs = draw_local_pairs(jax.random.fold_in(seeds[15], 71), 0)
    cross_x = draw_cross_x(jax.random.fold_in(seeds[15], 71), 0)
    cross_y = draw_cross_y(jax.random.fold_in(seeds[15], 71), 0)
    pair_counts = draw_pair_counts(jax.random.fold_in(seeds[15], 71), 0)
    w_rbf = scatter_about(seeds[7], (NRBF, HID), NRBF ** -0.5, 2.0)
    w_src = scatter_about(seeds[8], (FEAT, HID), FEAT ** -0.5, 0.75)
    w_dst = scatter_about(seeds[9], (FEAT, HID), FEAT ** -0.5, 0.75)
    species_src = scatter_about(seeds[10], (NSPEC, HID), 0.5, 3.0)
    species_dst = scatter_about(seeds[11], (NSPEC, HID), 0.5, 3.0)
    w_hidden = scatter_about(seeds[12], (HID, HID), HID ** -0.5, 0.375)
    w_latent = scatter_about(seeds[13], (HID, FEAT), HID ** -0.5, 0.375)
    w_energy = scatter_about(seeds[14], (FEAT,), FEAT ** -0.5, 0.75, (), jnp.float32)
    return {"positions": positions, "features": features, "halo_lists": halo_lists, "local_pairs": local_pairs, "cross_x": cross_x, "cross_y": cross_y, "pair_counts": pair_counts, "w_rbf": w_rbf, "w_src": w_src, "w_dst": w_dst, "species_src": species_src, "species_dst": species_dst, "w_hidden": w_hidden, "w_latent": w_latent, "w_energy": w_energy}


cutoff_radius = 6.0
block_edge = 6.0
softening = 0.1

def pair_energy(src_pos, src_feat, dst_pos, dst_feat, spec_src, spec_dst, live_mask, offset, weights):
    w_rbf, w_src, w_dst, species_src, species_dst, w_hidden, w_latent, w_energy = weights
    displace = dst_pos + offset[:, None] - src_pos
    radius = jnp.sqrt(lax.optimization_barrier(jnp.sum(displace * displace, axis=0)) + softening)
    orders = jnp.arange(1, w_rbf.shape[0] + 1).astype(jnp.float32)[:, None]
    basis = (jnp.sin(orders * (jnp.pi / cutoff_radius) * radius[None, :]) / radius[None, :]).astype(jnp.bfloat16)
    kinds = jnp.arange(species_src.shape[0], dtype=jnp.int32)[:, None]
    onehot_src = (spec_src[None, :] == kinds).astype(jnp.bfloat16)
    onehot_dst = (spec_dst[None, :] == kinds).astype(jnp.bfloat16)
    pre = jnp.dot(w_rbf.T, basis, preferred_element_type=jnp.float32)
    pre = pre + jnp.dot(w_src.T, src_feat.astype(jnp.bfloat16), preferred_element_type=jnp.float32)
    pre = pre + jnp.dot(w_dst.T, dst_feat.astype(jnp.bfloat16), preferred_element_type=jnp.float32)
    pre = pre + jnp.dot(species_src.T, onehot_src, preferred_element_type=jnp.float32)
    pre = pre + jnp.dot(species_dst.T, onehot_dst, preferred_element_type=jnp.float32)
    hidden = jax.nn.silu(pre).astype(jnp.bfloat16)
    second = jax.nn.silu(jnp.dot(w_hidden.T, hidden, preferred_element_type=jnp.float32)).astype(jnp.bfloat16)
    latent = jnp.dot(w_latent.T, second, preferred_element_type=jnp.float32)
    ratio = jnp.minimum(radius / cutoff_radius, 1.0)
    envelope = (1.0 - ratio ** 2) ** 2
    scores = jnp.dot(w_energy, latent, precision=lax.Precision.HIGHEST)
    return jnp.sum(envelope * scores * live_mask)

def block_grads(src_pos, src_feat, dst_pos, dst_feat, spec_src, spec_dst, live_mask, offset, weights):

    def energy_of(pos_one, feat_one, pos_two, feat_two):
        return pair_energy(pos_one, feat_one, pos_two, feat_two, spec_src, spec_dst, live_mask, offset, weights)
    energy, pullback = jax.vjp(energy_of, src_pos, src_feat.astype(jnp.float32), dst_pos, dst_feat.astype(jnp.float32))
    return (energy, pullback(jnp.ones_like(energy)))

def to_blocks(array):
    count = array.shape[-1] // BLOCK
    if array.ndim == 1:
        return array.reshape(count, BLOCK)
    return jnp.moveaxis(array.reshape(array.shape[0], count, BLOCK), 1, 0)

def from_blocks(array):
    return jnp.moveaxis(array, 0, 1).reshape(array.shape[1], -1)

def run_edges(src_pos, src_feat, dst_pos, dst_feat, spec_src, spec_dst, live_mask, offset, weights):
    inputs = tuple((to_blocks(item) for item in (src_pos, src_feat, dst_pos, dst_feat, spec_src, spec_dst, live_mask)))

    def visit(total, blocks):
        energy, grads = block_grads(*blocks, offset, weights)
        return (total + energy, grads)
    total, grads = lax.scan(visit, jnp.zeros((), jnp.float32), inputs)
    return (total, tuple((from_blocks(item) for item in grads)))

def device_work(operands, weights):
    positions, features, local_pairs, cross_x, cross_y, counts, recv_pos_x, recv_feat_x, recv_pos_y, recv_feat_y = operands
    zero_off = jnp.zeros((3,), jnp.float32)
    off_x = jnp.array([block_edge, 0.0, 0.0], jnp.float32)
    off_y = jnp.array([0.0, block_edge, 0.0], jnp.float32)
    slots_loc = jnp.arange(local_pairs.shape[1], dtype=jnp.int32)
    slots_cross = jnp.arange(cross_x.shape[1], dtype=jnp.int32)
    live_loc = (slots_loc < counts[0]).astype(jnp.float32)
    live_x = (slots_cross < counts[1]).astype(jnp.float32)
    live_y = (slots_cross < counts[2]).astype(jnp.float32)
    source, target = (local_pairs[0], local_pairs[1])
    energy_loc, grads = run_edges(positions[:, source], features[:, source], positions[:, target], features[:, target], local_pairs[2], local_pairs[3], live_loc, zero_off, weights)
    grad_pos = jnp.zeros(positions.shape, jnp.float32).at[:, source].add(grads[0]).at[:, target].add(grads[2])
    grad_feat = jnp.zeros(features.shape, jnp.float32).at[:, source].add(grads[1]).at[:, target].add(grads[3])
    halo_size = recv_pos_x.shape[1]
    outputs = []
    energies = energy_loc
    for pairs, recv_pos, recv_feat, live_mask, offset in ((cross_x, recv_pos_x, recv_feat_x, live_x, off_x), (cross_y, recv_pos_y, recv_feat_y, live_y, off_y)):
        source, slots = (pairs[0], pairs[1])
        energy, grads = run_edges(positions[:, source], features[:, source], recv_pos[:, slots], recv_feat[:, slots], pairs[2], pairs[3], live_mask, offset, weights)
        energies = energies + energy
        grad_pos = grad_pos.at[:, source].add(grads[0])
        grad_feat = grad_feat.at[:, source].add(grads[1])
        outputs.append(jnp.zeros((3, halo_size), jnp.float32).at[:, slots].add(grads[2]))
        outputs.append(jnp.zeros((features.shape[0], halo_size), jnp.float32).at[:, slots].add(grads[3]))
    return (energies, grad_pos, grad_feat, outputs[0], outputs[1], outputs[2], outputs[3])

def reference(positions, features, halo_lists, local_pairs, cross_x, cross_y, pair_counts, w_rbf, w_src, w_dst, species_src, species_dst, w_hidden, w_latent, w_energy):
    weights = (w_rbf, w_src, w_dst, species_src, species_dst, w_hidden, w_latent, w_energy)
    devices = N_GX * N_GY

    def per_device(array, width):
        return jnp.moveaxis(array.reshape(array.shape[0], devices, width), 1, 0)

    def grid(array):
        return array.reshape((N_GX, N_GY) + array.shape[1:])

    def flat(array):
        return array.reshape((devices,) + array.shape[2:])
    pick = jax.vmap(lambda table, index: table[:, index])
    scatter = jax.vmap(lambda total, index, extra: total.at[:, index].add(extra))
    pos_dev = per_device(positions, A_DEV)
    feat_dev = per_device(features, A_DEV)
    lists_dev = per_device(halo_lists, HALO)
    local_dev = per_device(local_pairs, E_LOC)
    xdev = per_device(cross_x, E_X)
    ydev = per_device(cross_y, E_X)
    recv_pos_x = flat(jnp.roll(grid(pick(pos_dev, lists_dev[:, 0])), -1, axis=0))
    recv_feat_x = flat(jnp.roll(grid(pick(feat_dev, lists_dev[:, 0])), -1, axis=0))
    recv_pos_y = flat(jnp.roll(grid(pick(pos_dev, lists_dev[:, 1])), -1, axis=1))
    recv_feat_y = flat(jnp.roll(grid(pick(feat_dev, lists_dev[:, 1])), -1, axis=1))
    results = lax.map(lambda operands: device_work(operands, weights), (pos_dev, feat_dev, local_dev, xdev, ydev, pair_counts, recv_pos_x, recv_feat_x, recv_pos_y, recv_feat_y))
    energies, grad_pos, grad_feat, hpos_x, hfeat_x, hpos_y, hfeat_y = results
    grad_pos = scatter(grad_pos, lists_dev[:, 0], flat(jnp.roll(grid(hpos_x), 1, axis=0)))
    grad_feat = scatter(grad_feat, lists_dev[:, 0], flat(jnp.roll(grid(hfeat_x), 1, axis=0)))
    grad_pos = scatter(grad_pos, lists_dev[:, 1], flat(jnp.roll(grid(hpos_y), 1, axis=1)))
    grad_feat = scatter(grad_feat, lists_dev[:, 1], flat(jnp.roll(grid(hfeat_y), 1, axis=1)))
    forces = -jnp.moveaxis(grad_pos, 0, 1).reshape(3, ATOMS)
    feature_grads = jnp.moveaxis(grad_feat, 0, 1).reshape(features.shape[0], ATOMS)
    energy = (jnp.sum(energies) / ATOMS).reshape(1)
    return (energy, forces, feature_grads)
```

```python
import functools
import math

import jax
import jax.numpy as jnp
from jax import lax
from jax.experimental import pallas as pl
from jax.experimental.pallas import tpu as pltpu
from jax.sharding import PartitionSpec as P

CUTOFF = 6.0
EDGE = 6.0
SOFT = 0.1
BLK = 512
LO = 256
ROWS = 80
F32 = jnp.float32
BF16 = jnp.bfloat16


def shifted(array, axis, by):
    length = lax.axis_size(axis)
    return lax.ppermute(array, axis, [(i, (i + by) % length) for i in range(length)])


def silu_parts(x):
    sig = 0.5 * jnp.tanh(0.5 * x) + 0.5
    y = x * sig
    return y, sig + y * (1.0 - sig)


def sin_cos_pi(y):
    whole = jnp.floor(y + 0.5)
    t = (y - whole) * math.pi
    odd = whole - 2.0 * jnp.floor(whole * 0.5)
    sign = 1.0 - 2.0 * odd
    t2 = t * t
    s = -1.0 / 39916800.0
    for c in (1.0 / 362880.0, -1.0 / 5040.0, 1.0 / 120.0, -1.0 / 6.0, 1.0):
        s = s * t2 + c
    c_ = 1.0 / 479001600.0
    for c in (-1.0 / 3628800.0, 1.0 / 40320.0, -1.0 / 720.0, 1.0 / 24.0, -0.5, 1.0):
        c_ = c_ * t2 + c
    return s * t * sign, c_ * sign


def lane_lookup(table, index):
    chunks = table.shape[1] // 128
    parts = []
    for g in range(index.shape[1] // 128):
        ix = index[:, g * 128 : (g + 1) * 128]
        lane = jnp.broadcast_to(ix & 127, (8, 128))
        row = jnp.broadcast_to(ix >> 7, (8, 128))
        val = jnp.take_along_axis(table[:, 0:128], lane, axis=1, mode="promise_in_bounds")
        for c in range(1, chunks):
            got = jnp.take_along_axis(
                table[:, c * 128 : (c + 1) * 128], lane, axis=1, mode="promise_in_bounds"
            )
            val = jnp.where(row == c, got, val)
        parts.append(val)
    return jnp.concatenate(parts, axis=1)


def one_hot(index):
    low = (index & (LO - 1)).astype(F32)
    rows = lax.broadcasted_iota(jnp.int32, (LO, index.shape[1]), 0).astype(F32)
    return jnp.where(rows == low, 1.0, 0.0).astype(BF16)


def fill_tables(features_ref, positions_ref, table, place):
    atoms = features_ref.shape[1]
    width = features_ref.shape[0]
    for h in range(atoms // LO):
        table[h * width : (h + 1) * width, :] = features_ref[:, h * LO : (h + 1) * LO]
    place[...] = jnp.zeros_like(place)
    place[0:3, :] = positions_ref[...]


def fill_weights(w_rbf, w_src, w_dst, species_src, species_dst, w_hidden, w_latent, w_energy, wt, wb, wht, vec):
    stack = jnp.concatenate(
        [
            w_src[...].astype(F32),
            w_dst[...].astype(F32),
            w_rbf[...].astype(F32),
            species_src[...].astype(F32),
            species_dst[...].astype(F32),
        ],
        axis=0,
    )
    wb[...] = stack.astype(BF16)
    wt[...] = stack.T.astype(BF16)
    wht[...] = w_hidden[...].astype(F32).T.astype(BF16)
    score = jnp.sum(w_latent[...].astype(F32) * w_energy[...], axis=1, keepdims=True)
    vec[...] = jnp.broadcast_to(score, vec.shape)


def pick(table, hot, index):
    width = 64
    got = jnp.dot(table, hot, preferred_element_type=F32)
    hi = index >> 8
    out = got[0:width]
    for h in range(1, table.shape[0] // width):
        out = jnp.where(hi == h, got[h * width : (h + 1) * width], out)
    return out


def spread(values, index, count):
    hi = index >> 8
    return jnp.concatenate(
        [jnp.where(hi == h, values, 0.0).astype(BF16) for h in range(count)], axis=0
    )


def scatter_product(wide, hot):
    return lax.dot_general(wide, hot, (((1,), (1,)), ((), ())), preferred_element_type=F32)


def pair_block(src, dst, kind_src, kind_dst, live, offset, table_i, place_i, table_j, place_j, weights):
    wt, wb, wht, w_hidden, vec = weights
    width = src.shape[1]
    ids = lax.broadcasted_iota(jnp.int32, (8, width), 0)
    ids_f = ids.astype(F32)
    at = lane_lookup(place_j[...], dst)
    if offset is not None:
        at = at + jnp.where(ids == offset, EDGE, 0.0)
    diff = at - lane_lookup(place_i[...], src)
    r = jnp.sqrt(jnp.sum(diff * diff, axis=0, keepdims=True) + SOFT)
    inv = 1.0 / r
    order = ids_f + 1.0
    sine, cosine = sin_cos_pi(order * (r * (1.0 / CUTOFF)))
    basis = sine * inv
    slope = (order * (math.pi / CUTOFF) * cosine - basis) * inv
    kinds = jnp.where(ids < 4, kind_src, kind_dst + 4)
    species = jnp.where(ids == kinds, 1.0, 0.0)
    hot_i = one_hot(src)
    hot_j = one_hot(dst)
    x = jnp.concatenate(
        [
            pick(table_i[...], hot_i, src).astype(BF16),
            pick(table_j[...], hot_j, dst).astype(BF16),
            jnp.concatenate([basis, species], axis=0).astype(BF16),
        ],
        axis=0,
    )
    pre = jnp.dot(wt[...], x, preferred_element_type=F32)
    hidden, slope_one = silu_parts(pre)
    pre_two = jnp.dot(wht[...], hidden.astype(BF16), preferred_element_type=F32)
    second, slope_two = silu_parts(pre_two)
    v = vec[...][:, 0:1]
    score = jnp.sum(second * v, axis=0, keepdims=True)
    back = jnp.dot(w_hidden[...], (slope_two * v).astype(BF16), preferred_element_type=F32)
    grad_x = jnp.dot(wb[...], (back * slope_one).astype(BF16), preferred_element_type=F32)
    ratio = jnp.minimum(r * (1.0 / CUTOFF), 1.0)
    rest = 1.0 - ratio * ratio
    envelope = rest * rest * live
    energy = envelope * score
    grad_x = grad_x * envelope
    grad_r = jnp.sum(grad_x[128:136] * slope, axis=0, keepdims=True)
    grad_r = grad_r + score * live * (rest * ratio * (-4.0 / CUTOFF))
    grad_d = diff * (grad_r * inv)
    coarse = grad_d.astype(BF16).astype(F32)
    fine = grad_d - coarse
    place = jnp.concatenate([coarse, fine], axis=0)
    grad_i = jnp.concatenate([grad_x[0:64], -place], axis=0)
    grad_j = jnp.concatenate([grad_x[64:128], place], axis=0)
    return energy, grad_i, grad_j, hot_i, hot_j


def unpack(acc, feat_ref, place_ref):
    width = feat_ref.shape[0]
    for h in range(acc.shape[0] // ROWS):
        cols = slice(h * LO, (h + 1) * LO)
        feat_ref[:, cols] = acc[h * ROWS : h * ROWS + width, :].astype(feat_ref.dtype)
        fine = acc[h * ROWS + width : h * ROWS + width + 8, :] + acc[h * ROWS + width + 8 : h * ROWS + width + 16, :]
        place_ref[:, cols] = fine[0:3]


def local_kernel(first, last_call, *refs):
    (counts, pairs, positions, features, acc_in, energy_in, w_rbf, w_src, w_dst, species_src, species_dst, w_hidden,
     w_latent, w_energy) = refs[:14]
    if last_call:
        feat_out, place_out, energy, table, place, wt, wb, wht, vec, acc = refs[14:]
    else:
        acc, energy, table, place, wt, wb, wht, vec = refs[14:]
    step = pl.program_id(0)
    spans = features.shape[1] // LO

    @pl.when(step == 0)
    def _():
        fill_tables(features, positions, table, place)
        fill_weights(w_rbf, w_src, w_dst, species_src, species_dst, w_hidden, w_latent, w_energy, wt, wb, wht, vec)
        acc[...] = acc_in[...]
        energy[...] = energy_in[...]

    base = (step + first) * BLK

    @pl.when(base < counts[0, 0])
    def _():
        src, dst = pairs[0:1, :], pairs[1:2, :]
        slot = base + lax.broadcasted_iota(jnp.int32, (1, BLK), 1)
        live = jnp.where(slot < counts[0, 0], 1.0, 0.0)
        e, grad_i, grad_j, hot_i, hot_j = pair_block(
            src, dst, pairs[2:3, :], pairs[3:4, :], live, None, table, place, table, place, (wt, wb, wht, w_hidden, vec)
        )
        energy[...] += e
        acc[...] += scatter_product(spread(grad_i, src, spans), hot_i) + scatter_product(spread(grad_j, dst, spans), hot_j)

    if last_call:

        @pl.when(step == pl.num_programs(0) - 1)
        def _():
            unpack(acc, feat_out, place_out)


def cross_kernel(blocks, *refs):
    (counts, pairs_x, pairs_y, positions, features, positions_x, features_x, list_x, positions_y, features_y, list_y,
     acc_in, energy_in, w_rbf, w_src, w_dst, species_src, species_dst, w_hidden, w_latent, w_energy) = refs[:21]
    acc, energy, feat_x, place_x, feat_y, place_y, table, place, table_n, place_n, slots, wt, wb, wht, vec, acc_n = refs[21:]
    step = pl.program_id(0)
    spans = features.shape[1] // LO

    @pl.when(step == 0)
    def _():
        fill_tables(features, positions, table, place)
        fill_weights(w_rbf, w_src, w_dst, species_src, species_dst, w_hidden, w_latent, w_energy, wt, wb, wht, vec)
        acc[...] = acc_in[...]
        energy[...] = energy_in[...]

    def side(axis, pairs, positions_n, features_n, list_n, feat_n, place_out):
        first = axis * blocks

        @pl.when(step == first)
        def _():
            fill_tables(features_n, positions_n, table_n, place_n)
            slots[...] = jnp.broadcast_to(list_n[axis : axis + 1, :], slots.shape)
            acc_n[...] = jnp.zeros_like(acc_n)

        base = (step - first) * BLK

        @pl.when((step >= first) & (step < first + blocks) & (base < counts[0, 1 + axis]))
        def _():
            src = pairs[0:1, :]
            dst = lane_lookup(slots[...], pairs[1:2, :])[0:1]
            slot = base + lax.broadcasted_iota(jnp.int32, (1, BLK), 1)
            live = jnp.where(slot < counts[0, 1 + axis], 1.0, 0.0)
            e, grad_i, grad_j, hot_i, hot_j = pair_block(
                src, dst, pairs[2:3, :], pairs[3:4, :], live, axis, table, place, table_n, place_n,
                (wt, wb, wht, w_hidden, vec),
            )
            energy[...] += e
            acc[...] += scatter_product(spread(grad_i, src, spans), hot_i)
            acc_n[...] += scatter_product(spread(grad_j, dst, spans), hot_j)

        @pl.when(step == first + blocks - 1)
        def _():
            unpack(acc_n, feat_n, place_out)

    side(0, pairs_x, positions_x, features_x, list_x, feat_x, place_x)
    side(1, pairs_y, positions_y, features_y, list_y, feat_y, place_y)


def whole(array):
    return pl.BlockSpec(array.shape, lambda i: (0,) * len(array.shape))


SMEM = pl.BlockSpec(memory_space=pltpu.SMEM)


def weight_scratch(hid):
    return [
        pltpu.VMEM((hid, 144), BF16),
        pltpu.VMEM((144, hid), BF16),
        pltpu.VMEM((hid, hid), BF16),
        pltpu.VMEM((hid, 128), F32),
    ]


def run_local(first, blocks, last_call, counts, pairs, positions, features, acc, energy, weights):
    width, atoms = features.shape
    rest = (positions, features, acc, energy) + weights
    if last_call:
        outs = [jax.ShapeDtypeStruct((width, atoms), F32), jax.ShapeDtypeStruct((3, atoms), F32), energy]
    else:
        outs = [acc, energy]
    scratch = [pltpu.VMEM((atoms // LO * width, LO), BF16), pltpu.VMEM((8, atoms), F32)] + weight_scratch(
        weights[0].shape[1]
    )
    if last_call:
        scratch.append(pltpu.VMEM(acc.shape, F32))
    return pl.pallas_call(
        functools.partial(local_kernel, first, last_call),
        grid=(blocks,),
        in_specs=[SMEM, pl.BlockSpec((4, BLK), lambda i: (0, i + first))] + [whole(a) for a in rest],
        out_specs=[whole(o) for o in outs],
        out_shape=[jax.ShapeDtypeStruct(o.shape, o.dtype) for o in outs],
        scratch_shapes=scratch,
        compiler_params=pltpu.CompilerParams(vmem_limit_bytes=50 * 1024 * 1024),
        cost_estimate=pl.CostEstimate(flops=blocks * 3000000000, bytes_accessed=2000000, transcendentals=0),
    )(counts, pairs, *rest)


def run_cross(counts, pairs_x, pairs_y, rest, width, atoms):
    blocks = pairs_x.shape[1] // BLK
    acc, energy = rest[8], rest[9]
    outs = [acc, energy] + [jax.ShapeDtypeStruct((width, atoms), BF16), jax.ShapeDtypeStruct((3, atoms), F32)] * 2
    hid = rest[10].shape[1]
    table = pltpu.VMEM((atoms // LO * width, LO), BF16)
    place = pltpu.VMEM((8, atoms), F32)
    return pl.pallas_call(
        functools.partial(cross_kernel, blocks),
        grid=(2 * blocks,),
        in_specs=[
            SMEM,
            pl.BlockSpec((4, BLK), lambda i: (0, jnp.minimum(i, blocks - 1))),
            pl.BlockSpec((4, BLK), lambda i: (0, jnp.maximum(i - blocks, 0))),
        ]
        + [whole(a) for a in rest],
        out_specs=[whole(o) for o in outs],
        out_shape=[jax.ShapeDtypeStruct(o.shape, o.dtype) for o in outs],
        scratch_shapes=[table, place, table, place, pltpu.VMEM((8, rest[4].shape[1]), jnp.int32)]
        + weight_scratch(hid)
        + [pltpu.VMEM(acc.shape, F32)],
        compiler_params=pltpu.CompilerParams(vmem_limit_bytes=50 * 1024 * 1024),
        cost_estimate=pl.CostEstimate(flops=2 * blocks * 3000000000, bytes_accessed=2000000, transcendentals=0),
    )(counts, pairs_x, pairs_y, *rest)


EARLY = 4


def on_device(
    positions, features, halo_lists, local_pairs, cross_x, cross_y, pair_counts,
    w_rbf, w_src, w_dst, species_src, species_dst, w_hidden, w_latent, w_energy,
):
    width, atoms = features.shape
    weights = (w_rbf, w_src, w_dst, species_src, species_dst, w_hidden, w_latent, w_energy.reshape(1, -1))
    got_x = tuple(shifted(a, "gx", -1) for a in (positions, features, halo_lists))
    got_y = tuple(shifted(a, "gy", -1) for a in (positions, features, halo_lists))
    acc = jnp.zeros((atoms // LO * ROWS, LO), F32)
    energy = jnp.zeros((1, BLK), F32)
    acc, energy = run_local(0, EARLY, False, pair_counts, local_pairs, positions, features, acc, energy, weights)
    acc, energy, feat_x, place_x, feat_y, place_y = run_cross(
        pair_counts, cross_x, cross_y, (positions, features) + got_x + got_y + (acc, energy) + weights, width, atoms
    )
    back_x = (shifted(feat_x, "gx", 1), shifted(place_x, "gx", 1))
    back_y = (shifted(feat_y, "gy", 1), shifted(place_y, "gy", 1))
    late = local_pairs.shape[1] // BLK - EARLY
    feat, place, energy = run_local(
        EARLY, late, True, pair_counts, local_pairs, positions, features, acc, energy, weights
    )
    total = lax.psum(jnp.sum(energy), ("gx", "gy"))
    atoms_all = atoms * lax.axis_size("gx") * lax.axis_size("gy")
    feat = feat + back_x[0].astype(F32) + back_y[0].astype(F32)
    place = place + back_x[1] + back_y[1]
    return (total / atoms_all).reshape(1), -place, feat


def solution(mesh):
    split = P(None, ("gx", "gy"))
    return jax.shard_map(
        on_device,
        mesh=mesh,
        in_specs=(split,) * 6 + (P(("gx", "gy"), None),) + (P(),) * 8,
        out_specs=(P(), split, split),
        check_vma=False,
    )
```

```python
import functools
import math

import jax
import jax.numpy as jnp
from jax import lax
from jax.experimental import pallas as pl
from jax.experimental.pallas import tpu as pltpu
from jax.sharding import PartitionSpec as P

CUTOFF = 6.0
EDGE = 6.0
SOFT = 0.1
BLK = 512
LO = 256
ROWS = 80
F32 = jnp.float32
BF16 = jnp.bfloat16


def silu_parts(x):
    sig = 0.5 * jnp.tanh(0.5 * x) + 0.5
    y = x * sig
    return y, sig + y * (1.0 - sig)


def sin_cos_pi(y):
    whole = jnp.floor(y + 0.5)
    t = (y - whole) * math.pi
    odd = whole - 2.0 * jnp.floor(whole * 0.5)
    sign = 1.0 - 2.0 * odd
    t2 = t * t
    s = -1.0 / 39916800.0
    for c in (1.0 / 362880.0, -1.0 / 5040.0, 1.0 / 120.0, -1.0 / 6.0, 1.0):
        s = s * t2 + c
    c_ = 1.0 / 479001600.0
    for c in (-1.0 / 3628800.0, 1.0 / 40320.0, -1.0 / 720.0, 1.0 / 24.0, -0.5, 1.0):
        c_ = c_ * t2 + c
    return s * t * sign, c_ * sign


def lane_lookup(table, index):
    chunks = table.shape[1] // 128
    parts = []
    for g in range(index.shape[1] // 128):
        ix = index[:, g * 128 : (g + 1) * 128]
        lane = jnp.broadcast_to(ix & 127, (8, 128))
        row = jnp.broadcast_to(ix >> 7, (8, 128))
        val = jnp.take_along_axis(table[:, 0:128], lane, axis=1, mode="promise_in_bounds")
        for c in range(1, chunks):
            got = jnp.take_along_axis(
                table[:, c * 128 : (c + 1) * 128], lane, axis=1, mode="promise_in_bounds"
            )
            val = jnp.where(row == c, got, val)
        parts.append(val)
    return jnp.concatenate(parts, axis=1)


def one_hot(index):
    low = (index & (LO - 1)).astype(F32)
    rows = lax.broadcasted_iota(jnp.int32, (LO, index.shape[1]), 0).astype(F32)
    return jnp.where(rows == low, 1.0, 0.0).astype(BF16)


def fill_weights(w_rbf, w_src, w_dst, species_src, species_dst, w_hidden, w_latent, w_energy, wt, wb, wht, vec):
    stack = jnp.concatenate(
        [
            w_src[...].astype(F32),
            w_dst[...].astype(F32),
            w_rbf[...].astype(F32),
            species_src[...].astype(F32),
            species_dst[...].astype(F32),
        ],
        axis=0,
    )
    wb[...] = stack.astype(BF16)
    wt[...] = stack.T.astype(BF16)
    wht[...] = w_hidden[...].astype(F32).T.astype(BF16)
    score = jnp.sum(w_latent[...].astype(F32) * w_energy[...], axis=1, keepdims=True)
    vec[...] = jnp.broadcast_to(score, vec.shape)


def pick(table, hot, index):
    width = 64
    got = jnp.dot(table, hot, preferred_element_type=F32)
    hi = index >> 8
    out = got[0:width]
    for h in range(1, table.shape[0] // width):
        out = jnp.where(hi == h, got[h * width : (h + 1) * width], out)
    return out


def spread(values, index, count):
    hi = index >> 8
    return jnp.concatenate(
        [jnp.where(hi == h, values, 0.0).astype(BF16) for h in range(count)], axis=0
    )


def scatter_product(wide, hot):
    return lax.dot_general(wide, hot, (((1,), (1,)), ((), ())), preferred_element_type=F32)


def pair_block(src, dst, kind_src, kind_dst, live, offset, table_i, place_i, table_j, place_j, weights):
    wt, wb, wht, w_hidden, vec = weights
    width = src.shape[1]
    ids = lax.broadcasted_iota(jnp.int32, (8, width), 0)
    ids_f = ids.astype(F32)
    at = lane_lookup(place_j[...], dst)
    if offset is not None:
        at = at + jnp.where(ids == offset, EDGE, 0.0)
    diff = jnp.where(ids < 3, at - lane_lookup(place_i[...], src), 0.0)
    r = jnp.sqrt(jnp.sum(diff * diff, axis=0, keepdims=True) + SOFT)
    inv = 1.0 / r
    order = ids_f + 1.0
    sine, cosine = sin_cos_pi(order * (r * (1.0 / CUTOFF)))
    basis = sine * inv
    slope = (order * (math.pi / CUTOFF) * cosine - basis) * inv
    kinds = jnp.where(ids < 4, kind_src, kind_dst + 4)
    species = jnp.where(ids == kinds, 1.0, 0.0)
    hot_i = one_hot(src)
    hot_j = one_hot(dst)
    x = jnp.concatenate(
        [
            pick(table_i[...], hot_i, src).astype(BF16),
            pick(table_j[...], hot_j, dst).astype(BF16),
            jnp.concatenate([basis, species], axis=0).astype(BF16),
        ],
        axis=0,
    )
    pre = jnp.dot(wt[...], x, preferred_element_type=F32)
    hidden, slope_one = silu_parts(pre)
    pre_two = jnp.dot(wht[...], hidden.astype(BF16), preferred_element_type=F32)
    second, slope_two = silu_parts(pre_two)
    v = vec[...][:, 0:1]
    score = jnp.sum(second * v, axis=0, keepdims=True)
    back = jnp.dot(w_hidden[...], (slope_two * v).astype(BF16), preferred_element_type=F32)
    grad_x = jnp.dot(wb[...], (back * slope_one).astype(BF16), preferred_element_type=F32)
    ratio = jnp.minimum(r * (1.0 / CUTOFF), 1.0)
    rest = 1.0 - ratio * ratio
    envelope = rest * rest * live
    energy = envelope * score
    grad_x = grad_x * envelope
    grad_r = jnp.sum(grad_x[128:136] * slope, axis=0, keepdims=True)
    grad_r = grad_r + score * live * (rest * ratio * (-4.0 / CUTOFF))
    grad_d = diff * (grad_r * inv)
    coarse = grad_d.astype(BF16).astype(F32)
    fine = grad_d - coarse
    place = jnp.concatenate([coarse, fine], axis=0)
    grad_i = jnp.concatenate([grad_x[0:64], -place], axis=0)
    grad_j = jnp.concatenate([grad_x[64:128], place], axis=0)
    return energy, grad_i, grad_j, hot_i, hot_j


def compact(acc, message):
    for h in range(acc.shape[0] // ROWS):
        top = h * ROWS
        place = acc[top + 64 : top + 72, :] + acc[top + 72 : top + 80, :]
        coarse = place.astype(BF16).astype(F32)
        rows = jnp.concatenate([acc[top : top + 64, :], coarse, place - coarse], axis=0)
        message[top : top + ROWS, :] = rows.astype(BF16)


def kernel(
    sizes, early, counts, local_pairs, pairs_x, pairs_y, positions, features, lists, w_rbf, w_src, w_dst, species_src,
    species_dst, w_hidden, w_latent, w_energy, energy_out, forces, feat_out, table, place, tables_n, places_n, wt, wb,
    wht, vec, acc, acc_n, message, message_n, energy, energy_one, energy_two, got_one, got_two, send_sem, recv_sem,
    send_one, recv_one, send_two, recv_two,
):
    n_gx, n_gy = sizes
    gx, gy = lax.axis_index("gx"), lax.axis_index("gy")
    width, atoms = features.shape
    spans = atoms // LO

    def peer(axis, by):
        if axis == 0:
            return (lax.rem(gx + by + n_gx, n_gx), gy)
        return (gx, lax.rem(gy + by + n_gy, n_gy))

    barrier = pltpu.get_barrier_semaphore()

    def greet(axis):
        def visit(by, carry):
            pl.semaphore_signal(barrier, inc=1, device_id=peer(axis, by), device_id_type=pl.DeviceIdType.MESH)
            return carry

        lax.fori_loop(1, sizes[axis], visit, 0)

    greet(0)
    greet(1)
    for h in range(spans):
        table[h * width : (h + 1) * width, :] = features[:, h * LO : (h + 1) * LO]
    place[...] = jnp.zeros_like(place)
    place[0:3, :] = positions[...]
    place[3:5, 0 : lists.shape[1]] = lists[...].astype(F32)
    pl.semaphore_wait(barrier, n_gx + n_gy - 2)

    def lend(axis, part, source, target, by):
        return pltpu.make_async_remote_copy(
            src_ref=source,
            dst_ref=target,
            send_sem=send_sem.at[axis, part],
            recv_sem=recv_sem.at[axis, part],
            device_id=peer(axis, by),
            device_id_type=pl.DeviceIdType.MESH,
        )

    halos = [
        (lend(axis, 0, table, tables_n.at[axis], -1), lend(axis, 1, place, places_n.at[axis], -1)) for axis in (0, 1)
    ]
    for pair in halos:
        for copy in pair:
            copy.start()
    fill_weights(w_rbf, w_src, w_dst, species_src, species_dst, w_hidden, w_latent, w_energy, wt, wb, wht, vec)
    acc[...] = jnp.zeros_like(acc)
    acc_n[...] = jnp.zeros_like(acc_n)
    energy[...] = jnp.zeros_like(energy)
    weights = (wt, wb, wht, w_hidden, vec)

    def columns(pairs, step, limit):
        base = pl.multiple_of(step * BLK, BLK)
        block = pairs[:, pl.ds(base, BLK)]
        slot = base + lax.broadcasted_iota(jnp.int32, (1, BLK), 1)
        live = jnp.where(slot < limit, 1.0, 0.0)
        return block[0:1], block[1:2], block[2:3], block[3:4], live

    def local_step(step, carry):
        src, dst, kind_src, kind_dst, live = columns(local_pairs, step, counts[0, 0])
        e, grad_i, grad_j, hot_i, hot_j = pair_block(
            src, dst, kind_src, kind_dst, live, None, table, place, table, place, weights
        )
        energy[...] += e
        acc[...] += scatter_product(spread(grad_i, src, spans), hot_i) + scatter_product(
            spread(grad_j, dst, spans), hot_j
        )
        return carry

    def cross_step(axis, pairs, step, carry):
        src, slots, kind_src, kind_dst, live = columns(pairs, step, counts[0, 1 + axis])
        place_n = places_n.at[axis]
        dst = lane_lookup(place_n[:, 0 : lists.shape[1]], slots)[3 + axis : 4 + axis].astype(jnp.int32)
        e, grad_i, grad_j, hot_i, hot_j = pair_block(
            src, dst, kind_src, kind_dst, live, axis, table, place, tables_n.at[axis], place_n, weights
        )
        energy[...] += e
        acc[...] += scatter_product(spread(grad_i, src, spans), hot_i)
        acc_n[axis] += scatter_product(spread(grad_j, dst, spans), hot_j)
        return carry

    lax.fori_loop(0, early, local_step, 0)
    returns = []
    for axis, pairs in ((0, pairs_x), (1, pairs_y)):
        for copy in halos[axis]:
            copy.wait_recv()
        lax.fori_loop(0, pairs.shape[1] // BLK, functools.partial(cross_step, axis, pairs), 0)
        compact(acc_n.at[axis], message.at[axis])
        back = lend(axis, 2, message.at[axis], message_n.at[axis], 1)
        back.start()
        returns.append(back)
    lax.fori_loop(early, local_pairs.shape[1] // BLK, local_step, 0)

    def exchange(axis, value, source, target, send, recv):
        count = sizes[axis]

        def copy_of(by):
            return pltpu.make_async_remote_copy(
                src_ref=source,
                dst_ref=target.at[by],
                send_sem=send.at[by],
                recv_sem=recv.at[by],
                device_id=peer(axis, by),
                device_id_type=pl.DeviceIdType.MESH,
            )

        def start(by, carry):
            copy_of(by).start()
            return carry

        def wait(by, carry):
            copy_of(by).wait()
            return carry

        source[...] = value
        lax.fori_loop(1, count, start, 0)
        return lambda: lax.fori_loop(1, count, wait, 0)

    total = jnp.broadcast_to(jnp.sum(energy[...], axis=1, keepdims=True), energy_one.shape)
    wait_one = exchange(1, total, energy_one, got_one, send_one, recv_one)
    wait_one()
    total = total + jnp.sum(got_one[1:n_gy], axis=0)
    wait_two = exchange(0, total, energy_two, got_two, send_two, recv_two)
    for pair in halos:
        for copy in pair:
            copy.wait_send()
    for back in returns:
        back.wait()
    for h in range(spans):
        top = h * ROWS
        cols = slice(h * LO, (h + 1) * LO)
        rows = acc[top : top + ROWS, :]
        for axis in (0, 1):
            rows = rows + message_n[axis, top : top + ROWS, :].astype(F32)
        feat_out[:, cols] = rows[0:width]
        forces[:, cols] = -(rows[width : width + 8] + rows[width + 8 : width + 16])[0:3]
    wait_two()
    total = total + jnp.sum(got_two[1:n_gx], axis=0)
    energy_out[...] = total[0:1, 0:1] / (atoms * n_gx * n_gy)


EARLY = 5


def on_device(
    positions, features, halo_lists, local_pairs, cross_x, cross_y, pair_counts,
    w_rbf, w_src, w_dst, species_src, species_dst, w_hidden, w_latent, w_energy,
):
    width, atoms = features.shape
    hid = w_hidden.shape[0]
    sizes = (lax.axis_size("gx"), lax.axis_size("gy"))
    spans = atoms // LO
    vmem = pl.BlockSpec(memory_space=pltpu.VMEM)
    dma = pltpu.SemaphoreType.DMA
    energy, forces, feat = pl.pallas_call(
        functools.partial(kernel, sizes, EARLY),
        in_specs=[pl.BlockSpec(memory_space=pltpu.SMEM)] + [vmem] * 14,
        out_specs=[vmem] * 3,
        out_shape=[
            jax.ShapeDtypeStruct((1, 1), F32),
            jax.ShapeDtypeStruct((3, atoms), F32),
            jax.ShapeDtypeStruct((width, atoms), F32),
        ],
        scratch_shapes=[
            pltpu.VMEM((spans * width, LO), BF16),
            pltpu.VMEM((8, atoms), F32),
            pltpu.VMEM((2, spans * width, LO), BF16),
            pltpu.VMEM((2, 8, atoms), F32),
            pltpu.VMEM((hid, 144), BF16),
            pltpu.VMEM((144, hid), BF16),
            pltpu.VMEM((hid, hid), BF16),
            pltpu.VMEM((hid, 128), F32),
            pltpu.VMEM((spans * ROWS, LO), F32),
            pltpu.VMEM((2, spans * ROWS, LO), F32),
            pltpu.VMEM((2, spans * ROWS, LO), BF16),
            pltpu.VMEM((2, spans * ROWS, LO), BF16),
            pltpu.VMEM((1, BLK), F32),
            pltpu.VMEM((8, 128), F32),
            pltpu.VMEM((8, 128), F32),
            pltpu.VMEM((sizes[1], 8, 128), F32),
            pltpu.VMEM((sizes[0], 8, 128), F32),
            dma((2, 3)),
            dma((2, 3)),
            dma((sizes[1],)),
            dma((sizes[1],)),
            dma((sizes[0],)),
            dma((sizes[0],)),
        ],
        compiler_params=pltpu.CompilerParams(
            collective_id=0, has_side_effects=True, vmem_limit_bytes=56 * 1024 * 1024
        ),
        cost_estimate=pl.CostEstimate(flops=60000000000, bytes_accessed=4000000, transcendentals=0),
    )(
        pair_counts, local_pairs, cross_x, cross_y, positions, features, halo_lists,
        w_rbf, w_src, w_dst, species_src, species_dst, w_hidden, w_latent, w_energy.reshape(1, -1),
    )
    return energy.reshape(1), forces, feat


def solution(mesh):
    split = P(None, ("gx", "gy"))
    return jax.shard_map(
        on_device,
        mesh=mesh,
        in_specs=(split,) * 6 + (P(("gx", "gy"), None),) + (P(),) * 8,
        out_specs=(P(), split, split),
        check_vma=False,
    )
```

```python
import functools
import math

import jax
import jax.numpy as jnp
from jax import lax
from jax.experimental import pallas as pl
from jax.experimental.pallas import tpu as pltpu
from jax.sharding import PartitionSpec as P

CUTOFF = 6.0
EDGE = 6.0
SOFT = 0.1
BLK = 1024
EARLY = 3
LO = 256
VMEM_LIMIT = 60 * 1024 * 1024
F32 = jnp.float32
BF16 = jnp.bfloat16
MESH = pl.DeviceIdType.MESH


def silu_parts(x):
    sig = 0.5 * jnp.tanh(0.5 * x) + 0.5
    y = x * sig
    return y, sig + y * (1.0 - sig)


def sin_cos_pi(y):
    whole = jnp.floor(y + 0.5)
    t = (y - whole) * math.pi
    odd = whole - 2.0 * jnp.floor(whole * 0.5)
    sign = 1.0 - 2.0 * odd
    t2 = t * t
    s = -1.0 / 39916800.0
    for c in (1.0 / 362880.0, -1.0 / 5040.0, 1.0 / 120.0, -1.0 / 6.0, 1.0):
        s = s * t2 + c
    c_ = 1.0 / 479001600.0
    for c in (-1.0 / 3628800.0, 1.0 / 40320.0, -1.0 / 720.0, 1.0 / 24.0, -0.5, 1.0):
        c_ = c_ * t2 + c
    return s * t * sign, c_ * sign


def lane_lookup(table, index):
    parts = []
    for g in range(index.shape[1] // 128):
        ix = index[:, g * 128 : (g + 1) * 128]
        lane = ix & 127
        chunk = ix >> 7
        val = None
        for c in range(table.shape[1] // 128):
            got = jnp.take_along_axis(
                table[:, c * 128 : (c + 1) * 128], lane, axis=1, mode="promise_in_bounds"
            )
            val = got if c == 0 else jnp.where(chunk == c, got, val)
        parts.append(val)
    return jnp.concatenate(parts, axis=1)


def one_hot(index):
    low = (index & (LO - 1)).astype(F32)
    rows = lax.broadcasted_iota(jnp.int32, (LO, index.shape[1]), 0).astype(F32)
    return jnp.where(rows == low, 1.0, 0.0).astype(BF16)


def pick(table, index, width):
    got = jnp.dot(table, one_hot(index), preferred_element_type=F32)
    hi = index >> 8
    out = got[0:width]
    for h in range(1, table.shape[0] // width):
        out = jnp.where(hi == h, got[h * width : (h + 1) * width], out)
    return out


def scatter_product(feat, place, index, spans):
    hi = index >> 8
    half = lax.broadcasted_iota(jnp.int32, place.shape, 0) >> 2
    parts = [jnp.where(hi == h, feat, 0.0).astype(BF16) for h in range(spans)]
    pairs = [jnp.where(hi == 2 * g + half, place, 0.0) for g in range(spans // 2)]
    parts.append(jnp.concatenate(pairs, axis=0).astype(BF16))
    wide = jnp.concatenate(parts, axis=0)
    return lax.dot_general(
        wide, one_hot(index), (((1,), (1,)), ((), ())), preferred_element_type=F32
    )


def fill_weights(refs, wt, wb, wht, vec):
    w_rbf, w_src, w_dst, species_src, species_dst, w_hidden, w_latent_t, w_energy = refs
    stack = jnp.concatenate(
        [a[...].astype(F32) for a in (w_src, w_dst, w_rbf, species_src, species_dst)], axis=0
    )
    wb[...] = stack.astype(BF16)
    wt[...] = stack.T.astype(BF16)
    wht[...] = w_hidden[...].astype(F32).T.astype(BF16)
    score = jnp.sum(w_latent_t[...].astype(F32).T * w_energy[...], axis=1, keepdims=True)
    vec[...] = jnp.broadcast_to(score, vec.shape)


def pair_block(first, second, kind_src, kind_dst, live, both, table_i, table_j, weights):
    wt, wb, wht, w_hidden, vec = weights
    width = first.shape[1]
    ids = lax.broadcasted_iota(jnp.int32, (8, width), 0)
    found = lane_lookup(both, jnp.where(ids < 4, first, second))
    target = found[7:8].astype(jnp.int32)
    diff = jnp.where(ids < 3, jnp.concatenate([found[4:8], found[0:4]], axis=0) - found, 0.0)
    r = jnp.sqrt(jnp.sum(diff * diff, axis=0, keepdims=True) + SOFT)
    inv = 1.0 / r
    order = ids.astype(F32) + 1.0
    sine, cosine = sin_cos_pi(order * (r * (1.0 / CUTOFF)))
    basis = sine * inv
    slope = (order * (math.pi / CUTOFF) * cosine - basis) * inv
    species = jnp.where(ids == jnp.where(ids < 4, kind_src, kind_dst + 4), 1.0, 0.0)
    feats = 64
    x = jnp.concatenate(
        [
            pick(table_i[...], first, feats).astype(BF16),
            pick(table_j[...], target, feats).astype(BF16),
            jnp.concatenate([basis, species], axis=0).astype(BF16),
        ],
        axis=0,
    )
    pre = jnp.dot(wt[...], x, preferred_element_type=F32)
    hidden, slope_one = silu_parts(pre)
    pre_two = jnp.dot(wht[...], hidden.astype(BF16), preferred_element_type=F32)
    top, slope_two = silu_parts(pre_two)
    v = vec[...][:, 0:1]
    score = jnp.sum(top * v, axis=0, keepdims=True)
    back = jnp.dot(w_hidden[...], (slope_two * v).astype(BF16), preferred_element_type=F32)
    grad_x = jnp.dot(wb[...], (back * slope_one).astype(BF16), preferred_element_type=F32)
    ratio = jnp.minimum(r * (1.0 / CUTOFF), 1.0)
    rest = 1.0 - ratio * ratio
    envelope = rest * rest * live
    grad_x = grad_x * envelope
    grad_r = jnp.sum(grad_x[2 * feats : 2 * feats + 8] * slope, axis=0, keepdims=True)
    grad_r = grad_r + score * live * (rest * ratio * (-4.0 / CUTOFF))
    grad_d = diff * (grad_r * inv)
    grad_d = grad_d + jnp.concatenate([grad_d[4:8], grad_d[0:4]], axis=0)
    return envelope * score, grad_x[0:feats], grad_x[feats : 2 * feats], grad_d, target


def kernel(
    sizes, counts, local_pairs, pairs_x, pairs_y, positions, features, lists, w_rbf, w_src, w_dst, species_src,
    species_dst, w_hidden, w_latent, w_energy, energy_out, sums_out, pairs, tables, lent, lent_n, both, wt, wb,
    wht, vec, acc_i, acc_j, message, message_n, hold_i, hold_j, hold_d, hold_ids, energy, energy_one, energy_two,
    got_one, got_two, send_sem, recv_sem, send_one, recv_one, send_two, recv_two,
):
    n_gx, n_gy = sizes
    gx, gy = lax.axis_index("gx"), lax.axis_index("gy")
    width, atoms = features.shape
    spans = atoms // LO
    halo = lists.shape[1]
    n_cross = pairs_x.shape[1] // BLK
    n_all = pairs.shape[1] // BLK
    start_x, start_y, start_late = EARLY, EARLY + n_cross, EARLY + 2 * n_cross

    def peer(axis, by):
        if axis == 0:
            return (lax.rem(gx + by + n_gx, n_gx), gy)
        return (gx, lax.rem(gy + by + n_gy, n_gy))

    barrier = pltpu.get_barrier_semaphore()
    for axis in (0, 1):

        def greet(by, carry):
            pl.semaphore_signal(barrier, inc=1, device_id=peer(axis, by), device_id_type=MESH)
            return carry

        lax.fori_loop(1, sizes[axis], greet, 0)

    early = EARLY * BLK
    pairs[:, 0:early] = local_pairs[:, 0:early]
    pairs[:, early : early + pairs_x.shape[1]] = pairs_x[...]
    pairs[:, early + pairs_x.shape[1] : start_late * BLK] = pairs_y[...]
    pairs[:, start_late * BLK :] = local_pairs[:, early:]
    for h in range(spans):
        tables[0, h * width : (h + 1) * width, :] = features[:, h * LO : (h + 1) * LO]
    place = positions[...]
    zero = jnp.zeros((1, atoms), F32)
    number = lax.broadcasted_iota(jnp.int32, (1, atoms), 1).astype(F32)
    both[0] = jnp.concatenate([place, zero, place, number], axis=0)
    for axis in (0, 1):
        picked = lane_lookup(both[0], jnp.broadcast_to(lists[axis : axis + 1, :], (8, halo)))
        lent[axis] = picked
    fill_weights(
        (w_rbf, w_src, w_dst, species_src, species_dst, w_hidden, w_latent, w_energy), wt, wb, wht, vec
    )
    acc_i[...] = jnp.zeros_like(acc_i)
    acc_j[...] = jnp.zeros_like(acc_j)
    energy[...] = jnp.zeros_like(energy)
    weights = (wt, wb, wht, w_hidden, vec)

    def lend(axis, part, source, target, by):
        return pltpu.make_async_remote_copy(
            src_ref=source,
            dst_ref=target,
            send_sem=send_sem.at[axis, part],
            recv_sem=recv_sem.at[axis, part],
            device_id=peer(axis, by),
            device_id_type=MESH,
        )

    halos = [
        (
            lend(axis, 0, tables.at[0], tables.at[axis + 1], -1),
            lend(axis, 1, lent.at[axis], lent_n.at[axis], -1),
        )
        for axis in (0, 1)
    ]
    returns = [lend(axis, 2, message.at[axis], message_n.at[axis], 1) for axis in (0, 1)]

    def side_of(step):
        cross = jnp.where(step < start_y, 1, 2)
        return jnp.where(step < start_x, 0, jnp.where(step < start_late, cross, 0))

    def network(step):
        side = side_of(step)
        skipped = jnp.where(
            side == 0, jnp.where(step < start_x, 0, 2 * n_cross), jnp.where(side == 1, start_x, start_y)
        )
        block = pairs[:, pl.ds(pl.multiple_of(step * BLK, BLK), BLK)]
        slot = (step - skipped) * BLK + lax.broadcasted_iota(jnp.int32, (1, BLK), 1)
        live = jnp.where(slot < counts[0, side], 1.0, 0.0)
        e, grad_i, grad_j, grad_d, target = pair_block(
            block[0:1], block[1:2], block[2:3], block[3:4], live, both[side], tables.at[0], tables.at[side], weights
        )
        energy[...] += e
        hold_i[...] = grad_i
        hold_j[...] = grad_j
        hold_d[...] = grad_d
        hold_ids[0:1, :] = block[0:1]
        hold_ids[1:2, :] = target

    def scatter(step):
        side = side_of(step)
        acc_i[...] += scatter_product(hold_i[...], -hold_d[...], hold_ids[0:1, :], spans)
        acc_j[side] += scatter_product(hold_j[...], hold_d[...], hold_ids[1:2, :], spans)

    network(0)
    pl.semaphore_wait(barrier, n_gx + n_gy - 2)
    for group in halos:
        for copy in group:
            copy.start()

    def visit(step, carry):
        for axis, begin in ((0, start_x), (1, start_y)):

            @pl.when(step == begin)
            def _():
                for copy in halos[axis]:
                    copy.wait_recv()
                ids = lax.broadcasted_iota(jnp.int32, (8, halo), 0)
                far = lent_n[axis] + jnp.where(ids == 4 + axis, EDGE, 0.0)
                both[axis + 1] = both[0]
                both[axis + 1, :, 0:halo] = jnp.where(ids < 4, both[0, :, 0:halo], far)

        scatter(step - 1)
        network(step)
        for axis, end in ((0, start_y), (1, start_late)):

            @pl.when(step == end)
            def _():
                message[axis] = acc_j[axis + 1].astype(BF16)
                returns[axis].start()

        return carry

    lax.fori_loop(1, n_all, visit, 0)

    def exchange(axis, value, source, target, send, recv):
        def copy_of(by):
            return pltpu.make_async_remote_copy(
                src_ref=source,
                dst_ref=target.at[by],
                send_sem=send.at[by],
                recv_sem=recv.at[by],
                device_id=peer(axis, by),
                device_id_type=MESH,
            )

        def start(by, carry):
            copy_of(by).start()
            return carry

        def wait(by, carry):
            copy_of(by).wait()
            return carry

        source[...] = value
        lax.fori_loop(1, sizes[axis], start, 0)
        return lambda: lax.fori_loop(1, sizes[axis], wait, 0)

    total = jnp.broadcast_to(jnp.sum(energy[...], axis=1, keepdims=True), energy_one.shape)
    wait_one = exchange(1, total, energy_one, got_one, send_one, recv_one)
    scatter(n_all - 1)
    wait_one()
    total = total + jnp.sum(got_one[1:n_gy], axis=0)
    wait_two = exchange(0, total, energy_two, got_two, send_two, recv_two)
    for group in halos:
        for copy in group:
            copy.wait_send()
    for back in returns:
        back.wait()
    sums_out[...] = acc_i[...] + acc_j[0] + message_n[0].astype(F32) + message_n[1].astype(F32)
    wait_two()
    total = total + jnp.sum(got_two[1:n_gx], axis=0)
    energy_out[...] = total[0:1, 0:1] / (atoms * n_gx * n_gy)


def finish(energy_in, sums, energy, forces, feat):
    width, atoms = feat.shape
    spans = atoms // LO
    energy[...] = energy_in[...]
    for h in range(spans):
        cols = slice(h * LO, (h + 1) * LO)
        rows = slice(h * width, (h + 1) * width)
        feat[:, cols] = sums[rows, :]
        top = spans * width + 4 * h
        forces[:, cols] = -sums[top : top + 3, :]


def on_device(
    positions, features, halo_lists, local_pairs, cross_x, cross_y, pair_counts,
    w_rbf, w_src, w_dst, species_src, species_dst, w_hidden, w_latent, w_energy,
):
    width, atoms = features.shape
    hid = w_hidden.shape[0]
    n_gx, n_gy = lax.axis_size("gx"), lax.axis_size("gy")
    spans = atoms // LO
    rows = spans * width + spans * 4
    halo = halo_lists.shape[1]
    slots = local_pairs.shape[1] + cross_x.shape[1] + cross_y.shape[1]
    vmem = pl.BlockSpec(memory_space=pltpu.VMEM)
    dma = pltpu.SemaphoreType.DMA
    sums = jax.ShapeDtypeStruct((rows, LO), F32)
    one = jax.ShapeDtypeStruct((1, 1), F32)
    partial = pl.pallas_call(
        functools.partial(kernel, (n_gx, n_gy)),
        in_specs=[pl.BlockSpec(memory_space=pltpu.SMEM)] + [vmem] * 14,
        out_specs=[vmem] * 2,
        out_shape=[one, sums],
        scratch_shapes=[
            pltpu.VMEM((4, slots), jnp.int32),
            pltpu.VMEM((3, spans * width, LO), BF16),
            pltpu.VMEM((2, 8, halo), F32),
            pltpu.VMEM((2, 8, halo), F32),
            pltpu.VMEM((3, 8, atoms), F32),
            pltpu.VMEM((hid, 144), BF16),
            pltpu.VMEM((144, hid), BF16),
            pltpu.VMEM((hid, hid), BF16),
            pltpu.VMEM((hid, 128), F32),
            pltpu.VMEM((rows, LO), F32),
            pltpu.VMEM((3, rows, LO), F32),
            pltpu.VMEM((2, rows, LO), BF16),
            pltpu.VMEM((2, rows, LO), BF16),
            pltpu.VMEM((width, BLK), F32),
            pltpu.VMEM((width, BLK), F32),
            pltpu.VMEM((8, BLK), F32),
            pltpu.VMEM((8, BLK), jnp.int32),
            pltpu.VMEM((1, BLK), F32),
            pltpu.VMEM((8, 128), F32),
            pltpu.VMEM((8, 128), F32),
            pltpu.VMEM((n_gy, 8, 128), F32),
            pltpu.VMEM((n_gx, 8, 128), F32),
            dma((2, 3)),
            dma((2, 3)),
            dma((n_gy,)),
            dma((n_gy,)),
            dma((n_gx,)),
            dma((n_gx,)),
        ],
        compiler_params=pltpu.CompilerParams(
            collective_id=0, has_side_effects=True, vmem_limit_bytes=VMEM_LIMIT
        ),
        cost_estimate=pl.CostEstimate(flops=30000000000, bytes_accessed=4000000, transcendentals=0),
    )(
        pair_counts, local_pairs, cross_x, cross_y, positions, features, halo_lists,
        w_rbf, w_src, w_dst, species_src, species_dst, w_hidden, w_latent.T, w_energy.reshape(1, -1),
    )
    energy, forces, feat = pl.pallas_call(
        finish,
        in_specs=[vmem] * 2,
        out_specs=[vmem] * 3,
        out_shape=[
            one,
            jax.ShapeDtypeStruct((3, atoms), F32),
            jax.ShapeDtypeStruct((width, atoms), F32),
        ],
        compiler_params=pltpu.CompilerParams(vmem_limit_bytes=VMEM_LIMIT),
        cost_estimate=pl.CostEstimate(flops=1000000, bytes_accessed=2000000, transcendentals=0),
    )(*partial)
    return energy.reshape(1), forces, feat


def solution(mesh):
    split = P(None, ("gx", "gy"))
    return jax.shard_map(
        on_device,
        mesh=mesh,
        in_specs=(split,) * 6 + (P(("gx", "gy"), None),) + (P(),) * 8,
        out_specs=(P(), split, split),
        check_vma=False,
    )
```

```python
import functools
import math

import jax
import jax.numpy as jnp
from jax import lax
from jax.experimental import pallas as pl
from jax.experimental.pallas import tpu as pltpu
from jax.sharding import PartitionSpec as P

CUTOFF = 6.0
EDGE = 6.0
SOFT = 0.1
BLK = 1024
EARLY = 4
PARTS = 1
CHUNK = 1024
DELAY = 1
LO = 256
VMEM_LIMIT = 60 * 1024 * 1024
F32 = jnp.float32
BF16 = jnp.bfloat16
MESH = pl.DeviceIdType.MESH


def silu_parts(x):
    sig = 0.5 * jnp.tanh(0.5 * x) + 0.5
    y = x * sig
    return y, sig + y * (1.0 - sig)


def sin_cos_pi(y):
    whole = jnp.floor(y + 0.5)
    t = (y - whole) * math.pi
    odd = whole - 2.0 * jnp.floor(whole * 0.5)
    sign = 1.0 - 2.0 * odd
    t2 = t * t
    s = -1.0 / 39916800.0
    for c in (1.0 / 362880.0, -1.0 / 5040.0, 1.0 / 120.0, -1.0 / 6.0, 1.0):
        s = s * t2 + c
    c_ = 1.0 / 479001600.0
    for c in (-1.0 / 3628800.0, 1.0 / 40320.0, -1.0 / 720.0, 1.0 / 24.0, -0.5, 1.0):
        c_ = c_ * t2 + c
    return s * t * sign, c_ * sign


def lane_lookup(table, index):
    parts = []
    for g in range(index.shape[1] // 128):
        ix = index[:, g * 128 : (g + 1) * 128]
        lane = ix & 127
        chunk = ix >> 7
        val = None
        for c in range(table.shape[1] // 128):
            got = jnp.take_along_axis(
                table[:, c * 128 : (c + 1) * 128], lane, axis=1, mode="promise_in_bounds"
            )
            val = got if c == 0 else jnp.where(chunk == c, got, val)
        parts.append(val)
    return jnp.concatenate(parts, axis=1)


def one_hot(index):
    low = (index & (LO - 1)).astype(F32)
    rows = lax.broadcasted_iota(jnp.int32, (LO, index.shape[1]), 0).astype(F32)
    return jnp.where(rows == low, 1.0, 0.0).astype(BF16)


def pick(table, index, width):
    got = jnp.dot(table, one_hot(index), preferred_element_type=F32)
    hi = index >> 8
    out = got[0:width]
    for h in range(1, table.shape[0] // width):
        out = jnp.where(hi == h, got[h * width : (h + 1) * width], out)
    return out


def scatter_product(feat, place, index, spans):
    hi = index >> 8
    half = lax.broadcasted_iota(jnp.int32, place.shape, 0) >> 2
    parts = [jnp.where(hi == h, feat, 0.0).astype(BF16) for h in range(spans)]
    pairs = [jnp.where(hi == 2 * g + half, place, 0.0) for g in range(spans // 2)]
    parts.append(jnp.concatenate(pairs, axis=0).astype(BF16))
    wide = jnp.concatenate(parts, axis=0)
    return lax.dot_general(
        wide, one_hot(index), (((1,), (1,)), ((), ())), preferred_element_type=F32
    )


def fill_weights(refs, wt, wb, wht, vec):
    w_rbf, w_src, w_dst, species_src, species_dst, w_hidden, w_latent_t, w_energy = refs
    stack = jnp.concatenate(
        [a[...].astype(F32) for a in (w_src, w_dst, w_rbf, species_src, species_dst)], axis=0
    )
    wb[...] = stack.astype(BF16)
    wt[...] = stack.T.astype(BF16)
    wht[...] = w_hidden[...].astype(F32).T.astype(BF16)
    score = jnp.sum(w_latent_t[...].astype(F32).T * w_energy[...], axis=1, keepdims=True)
    vec[...] = jnp.broadcast_to(score, vec.shape)


def pair_block(first, second, kind_src, kind_dst, live, both, table_i, table_j, weights):
    wt, wb, wht, w_hidden, vec = weights
    width = first.shape[1]
    feats = 64
    ids = lax.broadcasted_iota(jnp.int32, (8, width), 0)
    found = lane_lookup(both, jnp.where(ids < 4, first, second))
    target = found[7:8].astype(jnp.int32)
    yield None
    x_i = pick(table_i[...], first, feats).astype(BF16)
    yield None
    diff = jnp.where(ids < 3, jnp.concatenate([found[4:8], found[0:4]], axis=0) - found, 0.0)
    r = jnp.sqrt(jnp.sum(diff * diff, axis=0, keepdims=True) + SOFT)
    inv = 1.0 / r
    order = ids.astype(F32) + 1.0
    sine, cosine = sin_cos_pi(order * (r * (1.0 / CUTOFF)))
    basis = sine * inv
    slope = (order * (math.pi / CUTOFF) * cosine - basis) * inv
    species = jnp.where(ids == jnp.where(ids < 4, kind_src, kind_dst + 4), 1.0, 0.0)
    yield None
    x_j = pick(table_j[...], target, feats).astype(BF16)
    x = jnp.concatenate([x_i, x_j, jnp.concatenate([basis, species], axis=0).astype(BF16)], axis=0)
    yield None
    pre = jnp.dot(wt[...], x, preferred_element_type=F32)
    yield None
    hidden, slope_one = silu_parts(pre)
    hidden = hidden.astype(BF16)
    yield None
    pre_two = jnp.dot(wht[...], hidden, preferred_element_type=F32)
    yield None
    top, slope_two = silu_parts(pre_two)
    v = vec[...][:, 0:1]
    score = jnp.sum(top * v, axis=0, keepdims=True)
    down = (slope_two * v).astype(BF16)
    yield None
    back = jnp.dot(w_hidden[...], down, preferred_element_type=F32)
    yield None
    down = (back * slope_one).astype(BF16)
    yield None
    grad_x = jnp.dot(wb[...], down, preferred_element_type=F32)
    yield None
    ratio = jnp.minimum(r * (1.0 / CUTOFF), 1.0)
    rest = 1.0 - ratio * ratio
    envelope = rest * rest * live
    grad_x = grad_x * envelope
    grad_r = jnp.sum(grad_x[2 * feats : 2 * feats + 8] * slope, axis=0, keepdims=True)
    grad_r = grad_r + score * live * (rest * ratio * (-4.0 / CUTOFF))
    grad_d = diff * (grad_r * inv)
    grad_d = grad_d + jnp.concatenate([grad_d[4:8], grad_d[0:4]], axis=0)
    yield envelope * score, grad_x[0:feats], grad_x[feats : 2 * feats], grad_d, target


def kernel(
    sizes, counts, local_pairs, pairs_x, pairs_y, positions, features, lists, w_rbf, w_src, w_dst, species_src,
    species_dst, w_hidden, w_latent, w_energy, energy_out, sums_out, pairs, tables, lent, lent_n, both, wt, wb,
    wht, vec, acc_i, acc_j, message, message_n, hold_i, hold_j, hold_d, hold_ids, energy, energy_one, energy_two,
    got_one, got_two, send_sem, recv_sem, send_one, recv_one, send_two, recv_two,
):
    n_gx, n_gy = sizes
    gx, gy = lax.axis_index("gx"), lax.axis_index("gy")
    width, atoms = features.shape
    spans = atoms // LO
    halo = lists.shape[1]
    n_cross = pairs_x.shape[1] // BLK
    n_all = pairs.shape[1] // BLK
    start_x, start_y, start_late = EARLY, EARLY + n_cross, EARLY + 2 * n_cross

    def peer(axis, by):
        if axis == 0:
            return (lax.rem(gx + by + n_gx, n_gx), gy)
        return (gx, lax.rem(gy + by + n_gy, n_gy))

    barrier = pltpu.get_barrier_semaphore()
    for axis in (0, 1):

        def greet(by, carry):
            pl.semaphore_signal(barrier, inc=1, device_id=peer(axis, by), device_id_type=MESH)
            return carry

        lax.fori_loop(1, sizes[axis], greet, 0)

    early = EARLY * BLK
    pairs[:, 0:early] = local_pairs[:, 0:early]
    pairs[:, early : early + pairs_x.shape[1]] = pairs_x[...]
    pairs[:, early + pairs_x.shape[1] : start_late * BLK] = pairs_y[...]
    pairs[:, start_late * BLK :] = local_pairs[:, early:]
    for h in range(spans):
        tables[0, h * width : (h + 1) * width, :] = features[:, h * LO : (h + 1) * LO]
    place = positions[...]
    zero = jnp.zeros((1, atoms), F32)
    number = lax.broadcasted_iota(jnp.int32, (1, atoms), 1).astype(F32)
    both[0] = jnp.concatenate([place, zero, place, number], axis=0)
    for axis in (0, 1):
        picked = lane_lookup(both[0], jnp.broadcast_to(lists[axis : axis + 1, :], (8, halo)))
        lent[axis] = picked
    fill_weights(
        (w_rbf, w_src, w_dst, species_src, species_dst, w_hidden, w_latent, w_energy), wt, wb, wht, vec
    )
    acc_i[...] = jnp.zeros_like(acc_i)
    acc_j[...] = jnp.zeros_like(acc_j)
    energy[...] = jnp.zeros_like(energy)
    weights = (wt, wb, wht, w_hidden, vec)

    def lend(axis, part, source, target, by):
        return pltpu.make_async_remote_copy(
            src_ref=source,
            dst_ref=target,
            send_sem=send_sem.at[axis, part],
            recv_sem=recv_sem.at[axis, part],
            device_id=peer(axis, by),
            device_id_type=MESH,
        )

    halos = [
        (
            lend(axis, 0, tables.at[0], tables.at[axis + 1], -1),
            lend(axis, 1, lent.at[axis], lent_n.at[axis], -1),
        )
        for axis in (0, 1)
    ]
    returns = [lend(axis, 2, message.at[axis], message_n.at[axis], 1) for axis in (0, 1)]

    def side_of(step):
        cross = jnp.where(step < start_y, 1, 2)
        return jnp.where(step < start_x, 0, jnp.where(step < start_late, cross, 0))

    def network(step, part):
        size = BLK // PARTS
        side = side_of(step)
        skipped = jnp.where(
            side == 0, jnp.where(step < start_x, 0, 2 * n_cross), jnp.where(side == 1, start_x, start_y)
        )
        block = pairs[:, pl.ds(pl.multiple_of(step * BLK + part * size, size), size)]
        slot = (step - skipped) * BLK + part * size + lax.broadcasted_iota(jnp.int32, (1, size), 1)
        live = jnp.where(slot < counts[0, side], 1.0, 0.0)
        for got in pair_block(
            block[0:1], block[1:2], block[2:3], block[3:4], live, both[side], tables.at[0], tables.at[side], weights
        ):
            if got is None:
                yield
        yield
        cols = slice(part * size, (part + 1) * size)
        energy[:, cols] += got[0]
        hold_i[:, cols] = got[1]
        hold_j[:, cols] = got[2]
        hold_d[:, cols] = got[3]
        hold_ids[0:1, cols] = block[0:1]
        hold_ids[1:2, cols] = got[4]

    def scatter(step):
        side = side_of(step)
        for c in range(BLK // CHUNK):
            cols = slice(c * CHUNK, (c + 1) * CHUNK)
            acc_i[...] += scatter_product(hold_i[:, cols], -hold_d[:, cols], hold_ids[0:1, cols], spans)
            yield
            acc_j[side] += scatter_product(hold_j[:, cols], hold_d[:, cols], hold_ids[1:2, cols], spans)
            yield

    def turn(old, new):
        nets = [] if new is None else [network(new, part) for part in range(PARTS)]
        flows = nets + ([] if old is None else [scatter(old)])
        waits = [part * DELAY for part in range(len(nets))] + [0]
        left = list(zip(flows, waits))
        stages = 13
        done = {id(f): 0 for f in flows}
        for tick in range(100):
            for flow, wait in list(left):
                is_net = flow in nets
                if tick < wait or (is_net and done[id(flow)] == stages - 1):
                    continue
                done[id(flow)] += 1
                if next(flow, "end") == "end":
                    left.remove((flow, wait))
        for flow in nets:
            next(flow, None)

    pl.semaphore_wait(barrier, n_gx + n_gy - 2)
    for group in halos:
        for copy in group:
            copy.start()
    turn(None, 0)

    def visit(step, carry):
        for axis, begin in ((0, start_x), (1, start_y)):

            @pl.when(step == begin)
            def _():
                for copy in halos[axis]:
                    copy.wait_recv()
                ids = lax.broadcasted_iota(jnp.int32, (8, halo), 0)
                far = lent_n[axis] + jnp.where(ids == 4 + axis, EDGE, 0.0)
                both[axis + 1] = both[0]
                both[axis + 1, :, 0:halo] = jnp.where(ids < 4, both[0, :, 0:halo], far)

        turn(step - 1, step)
        for axis, end in ((0, start_y), (1, start_late)):

            @pl.when(step == end)
            def _():
                message[axis] = acc_j[axis + 1].astype(BF16)
                returns[axis].start()

        return carry

    lax.fori_loop(1, n_all, visit, 0)

    def exchange(axis, value, source, target, send, recv):
        def copy_of(by):
            return pltpu.make_async_remote_copy(
                src_ref=source,
                dst_ref=target.at[by],
                send_sem=send.at[by],
                recv_sem=recv.at[by],
                device_id=peer(axis, by),
                device_id_type=MESH,
            )

        def start(by, carry):
            copy_of(by).start()
            return carry

        def wait(by, carry):
            copy_of(by).wait()
            return carry

        source[...] = value
        lax.fori_loop(1, sizes[axis], start, 0)
        return lambda: lax.fori_loop(1, sizes[axis], wait, 0)

    total = jnp.broadcast_to(jnp.sum(energy[...], axis=1, keepdims=True), energy_one.shape)
    wait_one = exchange(1, total, energy_one, got_one, send_one, recv_one)
    turn(n_all - 1, None)
    wait_one()
    total = total + jnp.sum(got_one[1:n_gy], axis=0)
    wait_two = exchange(0, total, energy_two, got_two, send_two, recv_two)
    for group in halos:
        for copy in group:
            copy.wait_send()
    for back in returns:
        back.wait()
    sums_out[...] = acc_i[...] + acc_j[0] + message_n[0].astype(F32) + message_n[1].astype(F32)
    wait_two()
    total = total + jnp.sum(got_two[1:n_gx], axis=0)
    energy_out[...] = total[0:1, 0:1] / (atoms * n_gx * n_gy)


def finish(energy_in, sums, energy, forces, feat):
    width, atoms = feat.shape
    spans = atoms // LO
    energy[...] = energy_in[...]
    for h in range(spans):
        cols = slice(h * LO, (h + 1) * LO)
        rows = slice(h * width, (h + 1) * width)
        feat[:, cols] = sums[rows, :]
        top = spans * width + 4 * h
        forces[:, cols] = -sums[top : top + 3, :]


def on_device(
    positions, features, halo_lists, local_pairs, cross_x, cross_y, pair_counts,
    w_rbf, w_src, w_dst, species_src, species_dst, w_hidden, w_latent, w_energy,
):
    width, atoms = features.shape
    hid = w_hidden.shape[0]
    n_gx, n_gy = lax.axis_size("gx"), lax.axis_size("gy")
    spans = atoms // LO
    rows = spans * width + spans * 4
    halo = halo_lists.shape[1]
    slots = local_pairs.shape[1] + cross_x.shape[1] + cross_y.shape[1]
    vmem = pl.BlockSpec(memory_space=pltpu.VMEM)
    dma = pltpu.SemaphoreType.DMA
    sums = jax.ShapeDtypeStruct((rows, LO), F32)
    one = jax.ShapeDtypeStruct((1, 1), F32)
    partial = pl.pallas_call(
        functools.partial(kernel, (n_gx, n_gy)),
        in_specs=[pl.BlockSpec(memory_space=pltpu.SMEM)] + [vmem] * 14,
        out_specs=[vmem] * 2,
        out_shape=[one, sums],
        scratch_shapes=[
            pltpu.VMEM((4, slots), jnp.int32),
            pltpu.VMEM((3, spans * width, LO), BF16),
            pltpu.VMEM((2, 8, halo), F32),
            pltpu.VMEM((2, 8, halo), F32),
            pltpu.VMEM((3, 8, atoms), F32),
            pltpu.VMEM((hid, 144), BF16),
            pltpu.VMEM((144, hid), BF16),
            pltpu.VMEM((hid, hid), BF16),
            pltpu.VMEM((hid, 128), F32),
            pltpu.VMEM((rows, LO), F32),
            pltpu.VMEM((3, rows, LO), F32),
            pltpu.VMEM((2, rows, LO), BF16),
            pltpu.VMEM((2, rows, LO), BF16),
            pltpu.VMEM((width, BLK), F32),
            pltpu.VMEM((width, BLK), F32),
            pltpu.VMEM((8, BLK), F32),
            pltpu.VMEM((8, BLK), jnp.int32),
            pltpu.VMEM((1, BLK), F32),
            pltpu.VMEM((8, 128), F32),
            pltpu.VMEM((8, 128), F32),
            pltpu.VMEM((n_gy, 8, 128), F32),
            pltpu.VMEM((n_gx, 8, 128), F32),
            dma((2, 3)),
            dma((2, 3)),
            dma((n_gy,)),
            dma((n_gy,)),
            dma((n_gx,)),
            dma((n_gx,)),
        ],
        compiler_params=pltpu.CompilerParams(
            collective_id=0, has_side_effects=True, vmem_limit_bytes=VMEM_LIMIT
        ),
        cost_estimate=pl.CostEstimate(flops=30000000000, bytes_accessed=4000000, transcendentals=0),
    )(
        pair_counts, local_pairs, cross_x, cross_y, positions, features, halo_lists,
        w_rbf, w_src, w_dst, species_src, species_dst, w_hidden, w_latent.T, w_energy.reshape(1, -1),
    )
    energy, forces, feat = pl.pallas_call(
        finish,
        in_specs=[vmem] * 2,
        out_specs=[vmem] * 3,
        out_shape=[
            one,
            jax.ShapeDtypeStruct((3, atoms), F32),
            jax.ShapeDtypeStruct((width, atoms), F32),
        ],
        compiler_params=pltpu.CompilerParams(vmem_limit_bytes=VMEM_LIMIT),
        cost_estimate=pl.CostEstimate(flops=1000000, bytes_accessed=2000000, transcendentals=0),
    )(*partial)
    return energy.reshape(1), forces, feat


def solution(mesh):
    split = P(None, ("gx", "gy"))
    return jax.shard_map(
        on_device,
        mesh=mesh,
        in_specs=(split,) * 6 + (P(("gx", "gy"), None),) + (P(),) * 8,
        out_specs=(P(), split, split),
        check_vma=False,
    )
```

```python
import functools
import math

import jax
import jax.numpy as jnp
from jax import lax
from jax.experimental import pallas as pl
from jax.experimental.pallas import tpu as pltpu
from jax.sharding import PartitionSpec as P

CUTOFF = 6.0
EDGE = 6.0
SOFT = 0.1
BLK = 2048
LO = 256
VMEM_LIMIT = 60 * 1024 * 1024
F32 = jnp.float32
BF16 = jnp.bfloat16
MESH = pl.DeviceIdType.MESH


def silu_parts(x):
    sig = 0.5 * jnp.tanh(0.5 * x) + 0.5
    y = x * sig
    return y, sig + y * (1.0 - sig)


def sin_cos_pi(y):
    whole = jnp.floor(y + 0.5)
    t = (y - whole) * math.pi
    odd = whole - 2.0 * jnp.floor(whole * 0.5)
    sign = 1.0 - 2.0 * odd
    t2 = t * t
    s = -1.0 / 39916800.0
    for c in (1.0 / 362880.0, -1.0 / 5040.0, 1.0 / 120.0, -1.0 / 6.0, 1.0):
        s = s * t2 + c
    c_ = 1.0 / 479001600.0
    for c in (-1.0 / 3628800.0, 1.0 / 40320.0, -1.0 / 720.0, 1.0 / 24.0, -0.5, 1.0):
        c_ = c_ * t2 + c
    return s * t * sign, c_ * sign


def lane_lookup(table, index):
    parts = []
    for g in range(index.shape[1] // 128):
        ix = index[:, g * 128 : (g + 1) * 128]
        lane = ix & 127
        chunk = ix >> 7
        val = None
        for c in range(table.shape[1] // 128):
            got = jnp.take_along_axis(
                table[:, c * 128 : (c + 1) * 128], lane, axis=1, mode="promise_in_bounds"
            )
            val = got if c == 0 else jnp.where(chunk == c, got, val)
        parts.append(val)
    return jnp.concatenate(parts, axis=1)


def one_hot(index):
    low = (index & (LO - 1)).astype(F32)
    rows = lax.broadcasted_iota(jnp.int32, (LO, index.shape[1]), 0).astype(F32)
    return jnp.where(rows == low, 1.0, 0.0).astype(BF16)


def pick(table, index, width):
    got = jnp.dot(table, one_hot(index), preferred_element_type=F32)
    hi = index >> 8
    out = got[0:width]
    for h in range(1, table.shape[0] // width):
        out = jnp.where(hi == h, got[h * width : (h + 1) * width], out)
    return out


def scatter_product(feat, place, index, spans):
    hi = index >> 8
    half = lax.broadcasted_iota(jnp.int32, place.shape, 0) >> 2
    parts = [jnp.where(hi == h, feat, 0.0).astype(BF16) for h in range(spans)]
    pairs = [jnp.where(hi == 2 * g + half, place, 0.0) for g in range(spans // 2)]
    parts.append(jnp.concatenate(pairs, axis=0).astype(BF16))
    wide = jnp.concatenate(parts, axis=0)
    return lax.dot_general(
        wide, one_hot(index), (((1,), (1,)), ((), ())), preferred_element_type=F32
    )


def fill_weights(refs, wt, wb, wht, vec):
    w_rbf, w_src, w_dst, species_src, species_dst, w_hidden, w_latent_t, w_energy = refs
    stack = jnp.concatenate(
        [a[...].astype(F32) for a in (w_src, w_dst, w_rbf, species_src, species_dst)], axis=0
    )
    wb[...] = stack.astype(BF16)
    wt[...] = stack.T.astype(BF16)
    wht[...] = w_hidden[...].astype(F32).T.astype(BF16)
    score = jnp.sum(w_latent_t[...].astype(F32).T * w_energy[...], axis=1, keepdims=True)
    vec[...] = jnp.broadcast_to(score, vec.shape)


def forward(first, second, kind_src, kind_dst, live, both, table_i, table_j, weights):
    wt, wht, vec = weights
    feats = table_i.shape[0] * LO // both.shape[1]
    ids = lax.broadcasted_iota(jnp.int32, (8, first.shape[1]), 0)
    found = lane_lookup(both, jnp.where(ids < 4, first, second))
    target = found[7:8].astype(jnp.int32)
    diff = jnp.where(ids < 3, jnp.concatenate([found[4:8], found[0:4]], axis=0) - found, 0.0)
    r = jnp.sqrt(jnp.sum(diff * diff, axis=0, keepdims=True) + SOFT)
    inv = 1.0 / r
    order = ids.astype(F32) + 1.0
    sine, cosine = sin_cos_pi(order * (r * (1.0 / CUTOFF)))
    basis = sine * inv
    slope = (order * (math.pi / CUTOFF) * cosine - basis) * inv
    species = jnp.where(ids == jnp.where(ids < 4, kind_src, kind_dst + 4), 1.0, 0.0)
    x = jnp.concatenate(
        [
            pick(table_i[...], first, feats).astype(BF16),
            pick(table_j[...], target, feats).astype(BF16),
            jnp.concatenate([basis, species], axis=0).astype(BF16),
        ],
        axis=0,
    )
    hidden, slope_one = silu_parts(jnp.dot(wt[...], x, preferred_element_type=F32))
    top, slope_two = silu_parts(jnp.dot(wht[...], hidden.astype(BF16), preferred_element_type=F32))
    v = vec[...][:, 0:1]
    score = jnp.sum(top * v, axis=0, keepdims=True)
    ratio = jnp.minimum(r * (1.0 / CUTOFF), 1.0)
    rest = 1.0 - ratio * ratio
    envelope = rest * rest * live
    by_cutoff = score * live * (rest * ratio * (-4.0 / CUTOFF))
    way = diff * inv
    way = way + jnp.concatenate([way[4:8], way[0:4]], axis=0)
    return envelope * score, slope_one, (slope_two * v).astype(BF16), way, slope, envelope, by_cutoff, target


def backward(down, slope_one, way, slope, envelope, by_cutoff, w_hidden, wb, feats):
    back = jnp.dot(w_hidden, down, preferred_element_type=F32)
    grad_x = jnp.dot(wb, (back * slope_one).astype(BF16), preferred_element_type=F32) * envelope
    grad_r = jnp.sum(grad_x[2 * feats : 2 * feats + 8] * slope, axis=0, keepdims=True) + by_cutoff
    return grad_x[0:feats], grad_x[feats : 2 * feats], way * grad_r


def kernel(
    sizes, counts, local_pairs, pairs_x, pairs_y, positions, features, lists, w_rbf, w_src, w_dst, species_src,
    species_dst, w_hidden, w_latent, w_energy, energy_out, sums_out, pairs, tables, lent, lent_n, both, wt, wb,
    wht, vec, acc_i, acc_j, message, message_n, keep_slope, keep_down, keep_rows,
    keep_ids, hold_i, hold_j, hold_d, energy, energy_one, energy_two,
    got_one, got_two, send_sem, recv_sem, send_one, recv_one, send_two, recv_two,
):
    n_gx, n_gy = sizes
    gx, gy = lax.axis_index("gx"), lax.axis_index("gy")
    width, atoms = features.shape
    spans = atoms // LO
    halo = lists.shape[1]
    n_cross = pairs_x.shape[1] // BLK
    n_all = pairs.shape[1] // BLK
    start_x = local_pairs.shape[1] // BLK
    start_y = start_x + n_cross

    def peer(axis, by):
        if axis == 0:
            return (lax.rem(gx + by + n_gx, n_gx), gy)
        return (gx, lax.rem(gy + by + n_gy, n_gy))

    barrier = pltpu.get_barrier_semaphore()
    for axis in (0, 1):

        def greet(by, carry):
            pl.semaphore_signal(barrier, inc=1, device_id=peer(axis, by), device_id_type=MESH)
            return carry

        lax.fori_loop(1, sizes[axis], greet, 0)

    pairs[:, 0 : start_x * BLK] = local_pairs[...]
    pairs[:, start_x * BLK : start_y * BLK] = pairs_x[...]
    pairs[:, start_y * BLK :] = pairs_y[...]
    for h in range(spans):
        tables[0, h * width : (h + 1) * width, :] = features[:, h * LO : (h + 1) * LO]
    place = positions[...]
    zero = jnp.zeros((1, atoms), F32)
    number = lax.broadcasted_iota(jnp.int32, (1, atoms), 1).astype(F32)
    both[0] = jnp.concatenate([place, zero, place, number], axis=0)
    for axis in (0, 1):
        picked = lane_lookup(both[0], jnp.broadcast_to(lists[axis : axis + 1, :], (8, halo)))
        lent[axis] = picked
    fill_weights(
        (w_rbf, w_src, w_dst, species_src, species_dst, w_hidden, w_latent, w_energy), wt, wb, wht, vec
    )
    acc_i[...] = jnp.zeros_like(acc_i)
    acc_j[...] = jnp.zeros_like(acc_j)
    energy[...] = jnp.zeros_like(energy)

    def lend(axis, part, source, target, by):
        return pltpu.make_async_remote_copy(
            src_ref=source,
            dst_ref=target,
            send_sem=send_sem.at[axis, part],
            recv_sem=recv_sem.at[axis, part],
            device_id=peer(axis, by),
            device_id_type=MESH,
        )

    halos = [
        (
            lend(axis, 0, tables.at[0], tables.at[axis + 1], -1),
            lend(axis, 1, lent.at[axis], lent_n.at[axis], -1),
        )
        for axis in (0, 1)
    ]
    returns = [lend(axis, 2, message.at[axis], message_n.at[axis], 1) for axis in (0, 1)]

    def side_of(step):
        return jnp.where(step < start_x, 0, jnp.where(step < start_y, 1, 2))

    pl.semaphore_wait(barrier, n_gx + n_gy - 2)
    for group in halos:
        for copy in group:
            copy.start()

    def ahead(step, carry):
        for axis, begin in ((0, start_x), (1, start_y)):

            @pl.when(step == begin)
            def _():
                for copy in halos[axis]:
                    copy.wait_recv()
                ids = lax.broadcasted_iota(jnp.int32, (8, halo), 0)
                far = lent_n[axis] + jnp.where(ids == 4 + axis, EDGE, 0.0)
                both[axis + 1] = both[0]
                both[axis + 1, :, 0:halo] = jnp.where(ids < 4, both[0, :, 0:halo], far)

        side = side_of(step)
        skipped = jnp.where(side == 0, 0, jnp.where(side == 1, start_x, start_y))
        block = pairs[:, pl.ds(pl.multiple_of(step * BLK, BLK), BLK)]
        slot = (step - skipped) * BLK + lax.broadcasted_iota(jnp.int32, (1, BLK), 1)
        live = jnp.where(slot < counts[0, side], 1.0, 0.0)
        got = forward(
            block[0:1], block[1:2], block[2:3], block[3:4], live, both[side], tables.at[0], tables.at[side],
            (wt, wht, vec),
        )
        energy[...] += got[0]
        keep_slope[step] = got[1]
        keep_down[step] = got[2]
        keep_rows[step, 0:8] = got[3]
        keep_rows[step, 8:16] = got[4]
        keep_rows[step, 16:17] = got[5]
        keep_rows[step, 17:18] = got[6]
        keep_ids[step, 0:1] = block[0:1]
        keep_ids[step, 1:2] = got[7]
        return carry

    lax.fori_loop(0, n_all, ahead, 0)

    def exchange(axis, source, target, send, recv):
        def copy_of(by):
            return pltpu.make_async_remote_copy(
                src_ref=source,
                dst_ref=target.at[by],
                send_sem=send.at[by],
                recv_sem=recv.at[by],
                device_id=peer(axis, by),
                device_id_type=MESH,
            )

        def start(by, carry):
            copy_of(by).start()
            return carry

        def wait(by, carry):
            copy_of(by).wait()
            return carry

        return (
            lambda: lax.fori_loop(1, sizes[axis], start, 0),
            lambda: lax.fori_loop(1, sizes[axis], wait, 0),
        )

    start_one, wait_one = exchange(1, energy_one, got_one, send_one, recv_one)
    start_two, wait_two = exchange(0, energy_two, got_two, send_two, recv_two)
    energy_one[...] = jnp.broadcast_to(jnp.sum(energy[...], axis=1, keepdims=True), energy_one.shape)
    start_one()

    def place_of(turn):
        return jnp.where(turn < 2 * n_cross, start_x + turn, turn - 2 * n_cross)

    def network(turn):
        step = place_of(turn)
        rows = keep_rows[step]
        hold_i[...], hold_j[...], hold_d[...] = backward(
            keep_down[step], keep_slope[step], rows[0:8], rows[8:16], rows[16:17], rows[17:18], w_hidden[...], wb[...],
            width,
        )

    def scatter(turn):
        step = place_of(turn)
        ids = keep_ids[step]
        acc_i[...] += scatter_product(hold_i[...], -hold_d[...], ids[0:1], spans)
        acc_j[side_of(step)] += scatter_product(hold_j[...], hold_d[...], ids[1:2], spans)

    network(0)

    def behind(turn, carry):
        scatter(turn - 1)
        network(turn)
        for axis in (0, 1):

            @pl.when(turn == (axis + 1) * n_cross)
            def _():
                message[axis] = acc_j[axis + 1].astype(BF16)
                returns[axis].start()

        @pl.when(turn == n_all // 2)
        def _():
            wait_one()
            energy_two[...] = energy_one[...] + jnp.sum(got_one[1:n_gy], axis=0)
            start_two()

        return carry

    lax.fori_loop(1, n_all, behind, 0)
    scatter(n_all - 1)
    for group in halos:
        for copy in group:
            copy.wait_send()
    for back in returns:
        back.wait()
    sums_out[...] = acc_i[...] + acc_j[0] + message_n[0].astype(F32) + message_n[1].astype(F32)
    wait_two()
    total = energy_two[...] + jnp.sum(got_two[1:n_gx], axis=0)
    energy_out[...] = total[0:1, 0:1] / (atoms * n_gx * n_gy)


def finish(energy_in, sums, energy, forces, feat):
    width, atoms = feat.shape
    spans = atoms // LO
    energy[...] = energy_in[...]
    for h in range(spans):
        cols = slice(h * LO, (h + 1) * LO)
        rows = slice(h * width, (h + 1) * width)
        feat[:, cols] = sums[rows, :]
        top = spans * width + 4 * h
        forces[:, cols] = -sums[top : top + 3, :]


def on_device(
    positions, features, halo_lists, local_pairs, cross_x, cross_y, pair_counts,
    w_rbf, w_src, w_dst, species_src, species_dst, w_hidden, w_latent, w_energy,
):
    width, atoms = features.shape
    hid = w_hidden.shape[0]
    n_gx, n_gy = lax.axis_size("gx"), lax.axis_size("gy")
    spans = atoms // LO
    rows = spans * width + spans * 4
    halo = halo_lists.shape[1]
    slots = local_pairs.shape[1] + cross_x.shape[1] + cross_y.shape[1]
    vmem = pl.BlockSpec(memory_space=pltpu.VMEM)
    dma = pltpu.SemaphoreType.DMA
    sums = jax.ShapeDtypeStruct((rows, LO), F32)
    one = jax.ShapeDtypeStruct((1, 1), F32)
    partial = pl.pallas_call(
        functools.partial(kernel, (n_gx, n_gy)),
        in_specs=[pl.BlockSpec(memory_space=pltpu.SMEM)] + [vmem] * 14,
        out_specs=[vmem] * 2,
        out_shape=[one, sums],
        scratch_shapes=[
            pltpu.VMEM((4, slots), jnp.int32),
            pltpu.VMEM((3, spans * width, LO), BF16),
            pltpu.VMEM((2, 8, halo), F32),
            pltpu.VMEM((2, 8, halo), F32),
            pltpu.VMEM((3, 8, atoms), F32),
            pltpu.VMEM((hid, 144), BF16),
            pltpu.VMEM((144, hid), BF16),
            pltpu.VMEM((hid, hid), BF16),
            pltpu.VMEM((hid, 128), F32),
            pltpu.VMEM((rows, LO), F32),
            pltpu.VMEM((3, rows, LO), F32),
            pltpu.VMEM((2, rows, LO), BF16),
            pltpu.VMEM((2, rows, LO), BF16),
            pltpu.VMEM((slots // BLK, hid, BLK), F32),
            pltpu.VMEM((slots // BLK, hid, BLK), BF16),
            pltpu.VMEM((slots // BLK, 24, BLK), F32),
            pltpu.VMEM((slots // BLK, 8, BLK), jnp.int32),
            pltpu.VMEM((width, BLK), F32),
            pltpu.VMEM((width, BLK), F32),
            pltpu.VMEM((8, BLK), F32),
            pltpu.VMEM((1, BLK), F32),
            pltpu.VMEM((1, 128), F32),
            pltpu.VMEM((1, 128), F32),
            pltpu.VMEM((n_gy, 1, 128), F32),
            pltpu.VMEM((n_gx, 1, 128), F32),
            dma((2, 3)),
            dma((2, 3)),
            dma((n_gy,)),
            dma((n_gy,)),
            dma((n_gx,)),
            dma((n_gx,)),
        ],
        compiler_params=pltpu.CompilerParams(
            collective_id=0, has_side_effects=True, vmem_limit_bytes=VMEM_LIMIT
        ),
        cost_estimate=pl.CostEstimate(flops=30000000000, bytes_accessed=4000000, transcendentals=0),
    )(
        pair_counts, local_pairs, cross_x, cross_y, positions, features, halo_lists,
        w_rbf, w_src, w_dst, species_src, species_dst, w_hidden, w_latent.T, w_energy.reshape(1, -1),
    )
    energy, forces, feat = pl.pallas_call(
        finish,
        in_specs=[vmem] * 2,
        out_specs=[vmem] * 3,
        out_shape=[
            one,
            jax.ShapeDtypeStruct((3, atoms), F32),
            jax.ShapeDtypeStruct((width, atoms), F32),
        ],
        compiler_params=pltpu.CompilerParams(vmem_limit_bytes=VMEM_LIMIT),
        cost_estimate=pl.CostEstimate(flops=1000000, bytes_accessed=2000000, transcendentals=0),
    )(*partial)
    return energy.reshape(1), forces, feat


def solution(mesh):
    split = P(None, ("gx", "gy"))
    return jax.shard_map(
        on_device,
        mesh=mesh,
        in_specs=(split,) * 6 + (P(("gx", "gy"), None),) + (P(),) * 8,
        out_specs=(P(), split, split),
        check_vma=False,
    )
```

```python
import functools
import math

import jax
import jax.numpy as jnp
from jax import lax
from jax.experimental import pallas as pl
from jax.experimental.pallas import tpu as pltpu
from jax.sharding import PartitionSpec as P

CUTOFF = 6.0
EDGE = 6.0
SOFT = 0.1
BLK = 2048
LO = 256
VMEM_LIMIT = 60 * 1024 * 1024
F32 = jnp.float32
BF16 = jnp.bfloat16
MESH = pl.DeviceIdType.MESH


def silu_parts(z):
    u = jnp.tanh(z) + 1.0
    y = z * u
    return y, u + y * (2.0 - u)


def sin_cos_pi(y):
    whole = jnp.floor(y + 0.5)
    t = (y - whole) * math.pi
    odd = whole - 2.0 * jnp.floor(whole * 0.5)
    sign = 1.0 - 2.0 * odd
    t2 = t * t
    s = -1.0 / 39916800.0
    for c in (1.0 / 362880.0, -1.0 / 5040.0, 1.0 / 120.0, -1.0 / 6.0, 1.0):
        s = s * t2 + c
    c_ = 1.0 / 479001600.0
    for c in (-1.0 / 3628800.0, 1.0 / 40320.0, -1.0 / 720.0, 1.0 / 24.0, -0.5, 1.0):
        c_ = c_ * t2 + c
    return s * t * sign, c_ * sign


def lane_lookup(table, index):
    parts = []
    for g in range(index.shape[1] // 128):
        ix = index[:, g * 128 : (g + 1) * 128]
        lane = ix & 127
        chunk = ix >> 7
        val = None
        for c in range(table.shape[1] // 128):
            got = jnp.take_along_axis(
                table[:, c * 128 : (c + 1) * 128], lane, axis=1, mode="promise_in_bounds"
            )
            val = got if c == 0 else jnp.where(chunk == c, got, val)
        parts.append(val)
    return jnp.concatenate(parts, axis=1)


def one_hot(index):
    low = (index & (LO - 1)).astype(F32)
    rows = lax.broadcasted_iota(jnp.int32, (LO, index.shape[1]), 0).astype(F32)
    return jnp.where(rows == low, 1.0, 0.0).astype(BF16)


def pick(table, index, width):
    got = jnp.dot(table, one_hot(index), preferred_element_type=F32)
    hi = index >> 8
    out = got[0:width]
    for h in range(1, table.shape[0] // width):
        out = jnp.where(hi == h, got[h * width : (h + 1) * width], out)
    return out


def scatter_product(feat, place, index, spans):
    hi = index >> 8
    half = lax.broadcasted_iota(jnp.int32, place.shape, 0) >> 2
    parts = [jnp.where(hi == h, feat, 0.0).astype(BF16) for h in range(spans)]
    pairs = [jnp.where(hi == 2 * g + half, place, 0.0) for g in range(spans // 2)]
    parts.append(jnp.concatenate(pairs, axis=0).astype(BF16))
    wide = jnp.concatenate(parts, axis=0)
    return lax.dot_general(
        wide, one_hot(index), (((1,), (1,)), ((), ())), preferred_element_type=F32
    )


def fill_weights(refs, wt, wb, wht, vec):
    w_rbf, w_src, w_dst, species_src, species_dst, w_hidden, w_latent_t, w_energy = refs
    stack = jnp.concatenate(
        [a[...].astype(F32) for a in (w_src, w_dst, w_rbf, species_src, species_dst)], axis=0
    )
    wb[...] = (stack * 0.25).astype(BF16)
    wt[...] = (stack * 0.5).T.astype(BF16)
    wht[...] = (w_hidden[...].astype(F32) * 0.5).T.astype(BF16)
    score = jnp.sum(w_latent_t[...].astype(F32).T * w_energy[...], axis=1, keepdims=True)
    vec[...] = jnp.broadcast_to(score, vec.shape)


def forward(first, second, kind_src, kind_dst, live, both, table_i, table_j, weights):
    wt, wht, vec = weights
    feats = table_i.shape[0] * LO // both.shape[1]
    ids = lax.broadcasted_iota(jnp.int32, (8, first.shape[1]), 0)
    found = lane_lookup(both, jnp.where(ids < 4, first, second))
    target = found[7:8].astype(jnp.int32)
    diff = jnp.where(ids < 3, jnp.concatenate([found[4:8], found[0:4]], axis=0) - found, 0.0)
    r = jnp.sqrt(jnp.sum(diff * diff, axis=0, keepdims=True) + SOFT)
    inv = 1.0 / r
    order = ids.astype(F32) + 1.0
    sine, cosine = sin_cos_pi(order * (r * (1.0 / CUTOFF)))
    basis = sine * inv
    slope = (order * (math.pi / CUTOFF) * cosine - basis) * inv
    species = jnp.where(ids == jnp.where(ids < 4, kind_src, kind_dst + 4), 1.0, 0.0)
    x = jnp.concatenate(
        [
            pick(table_i[...], first, feats).astype(BF16),
            pick(table_j[...], target, feats).astype(BF16),
            jnp.concatenate([basis, species], axis=0).astype(BF16),
        ],
        axis=0,
    )
    hidden, slope_one = silu_parts(jnp.dot(wt[...], x, preferred_element_type=F32))
    half = jnp.dot(wht[...], hidden.astype(BF16), preferred_element_type=F32)
    u = jnp.tanh(half) + 1.0
    scaled = u * vec[...][:, 0:1]
    top = half * scaled
    score = jnp.sum(top, axis=0, keepdims=True)
    down = (scaled + top * (2.0 - u)).astype(BF16)
    ratio = jnp.minimum(r * (1.0 / CUTOFF), 1.0)
    rest = 1.0 - ratio * ratio
    envelope = rest * rest * live
    by_cutoff = score * live * (rest * ratio * (-4.0 / CUTOFF))
    way = diff * inv
    way = way + jnp.concatenate([way[4:8], way[0:4]], axis=0)
    return envelope * score, slope_one, down, way, slope, envelope, by_cutoff, target


def backward(down, slope_one, way, slope, envelope, by_cutoff, w_hidden, wb, feats):
    back = jnp.dot(w_hidden, down, preferred_element_type=F32)
    grad_x = jnp.dot(wb, (back * slope_one).astype(BF16), preferred_element_type=F32) * envelope
    grad_r = jnp.sum(grad_x[2 * feats : 2 * feats + 8] * slope, axis=0, keepdims=True) + by_cutoff
    return grad_x[0:feats], grad_x[feats : 2 * feats], way * grad_r


def kernel(
    sizes, counts, local_pairs, pairs_x, pairs_y, positions, features, lists, w_rbf, w_src, w_dst, species_src,
    species_dst, w_hidden, w_latent, w_energy, energy_out, sums_out, pairs, tables, lent, lent_n, both, wt, wb,
    wht, vec, acc_i, acc_j, message, message_n, keep_slope, keep_down, keep_rows,
    keep_ids, hold_i, hold_j, hold_d, energy, energy_one, energy_two,
    got_one, got_two, send_sem, recv_sem, send_one, recv_one, send_two, recv_two,
):
    n_gx, n_gy = sizes
    gx, gy = lax.axis_index("gx"), lax.axis_index("gy")
    width, atoms = features.shape
    spans = atoms // LO
    halo = lists.shape[1]
    n_cross = pairs_x.shape[1] // BLK
    n_all = pairs.shape[1] // BLK
    start_x = local_pairs.shape[1] // BLK
    start_y = start_x + n_cross

    def peer(axis, by):
        if axis == 0:
            return (lax.rem(gx + by + n_gx, n_gx), gy)
        return (gx, lax.rem(gy + by + n_gy, n_gy))

    barrier = pltpu.get_barrier_semaphore()
    for axis in (0, 1):

        def greet(by, carry):
            pl.semaphore_signal(barrier, inc=1, device_id=peer(axis, by), device_id_type=MESH)
            return carry

        lax.fori_loop(1, sizes[axis], greet, 0)

    pairs[:, 0 : start_x * BLK] = local_pairs[...]
    pairs[:, start_x * BLK : start_y * BLK] = pairs_x[...]
    pairs[:, start_y * BLK :] = pairs_y[...]
    for h in range(spans):
        tables[0, h * width : (h + 1) * width, :] = features[:, h * LO : (h + 1) * LO]
    place = positions[...]
    zero = jnp.zeros((1, atoms), F32)
    number = lax.broadcasted_iota(jnp.int32, (1, atoms), 1).astype(F32)
    both[0] = jnp.concatenate([place, zero, place, number], axis=0)
    for axis in (0, 1):
        picked = lane_lookup(both[0], jnp.broadcast_to(lists[axis : axis + 1, :], (8, halo)))
        lent[axis] = picked
    fill_weights(
        (w_rbf, w_src, w_dst, species_src, species_dst, w_hidden, w_latent, w_energy), wt, wb, wht, vec
    )
    acc_i[...] = jnp.zeros_like(acc_i)
    acc_j[...] = jnp.zeros_like(acc_j)
    energy[...] = jnp.zeros_like(energy)

    def lend(axis, part, source, target, by):
        return pltpu.make_async_remote_copy(
            src_ref=source,
            dst_ref=target,
            send_sem=send_sem.at[axis, part],
            recv_sem=recv_sem.at[axis, part],
            device_id=peer(axis, by),
            device_id_type=MESH,
        )

    halos = [
        (
            lend(axis, 0, tables.at[0], tables.at[axis + 1], -1),
            lend(axis, 1, lent.at[axis], lent_n.at[axis], -1),
        )
        for axis in (0, 1)
    ]
    returns = [lend(axis, 2, message.at[axis], message_n.at[axis], 1) for axis in (0, 1)]

    def side_of(step):
        return jnp.where(step < start_x, 0, jnp.where(step < start_y, 1, 2))

    pl.semaphore_wait(barrier, n_gx + n_gy - 2)
    for group in halos:
        for copy in group:
            copy.start()

    def ahead(step, carry):
        for axis, begin in ((0, start_x), (1, start_y)):

            @pl.when(step == begin)
            def _():
                for copy in halos[axis]:
                    copy.wait_recv()
                ids = lax.broadcasted_iota(jnp.int32, (8, halo), 0)
                far = lent_n[axis] + jnp.where(ids == 4 + axis, EDGE, 0.0)
                both[axis + 1] = both[0]
                both[axis + 1, :, 0:halo] = jnp.where(ids < 4, both[0, :, 0:halo], far)

        side = side_of(step)
        skipped = jnp.where(side == 0, 0, jnp.where(side == 1, start_x, start_y))
        block = pairs[:, pl.ds(pl.multiple_of(step * BLK, BLK), BLK)]
        slot = (step - skipped) * BLK + lax.broadcasted_iota(jnp.int32, (1, BLK), 1)
        live = jnp.where(slot < counts[0, side], 1.0, 0.0)
        got = forward(
            block[0:1], block[1:2], block[2:3], block[3:4], live, both[side], tables.at[0], tables.at[side],
            (wt, wht, vec),
        )
        energy[...] += got[0]
        keep_slope[step] = got[1]
        keep_down[step] = got[2]
        keep_rows[step, 0:8] = got[3]
        keep_rows[step, 8:16] = got[4]
        keep_rows[step, 16:17] = got[5]
        keep_rows[step, 17:18] = got[6]
        keep_ids[step, 0:1] = block[0:1]
        keep_ids[step, 1:2] = got[7]
        return carry

    lax.fori_loop(0, n_all, ahead, 0)

    def exchange(axis, source, target, send, recv):
        def copy_of(by):
            return pltpu.make_async_remote_copy(
                src_ref=source,
                dst_ref=target.at[by],
                send_sem=send.at[by],
                recv_sem=recv.at[by],
                device_id=peer(axis, by),
                device_id_type=MESH,
            )

        def start(by, carry):
            copy_of(by).start()
            return carry

        def wait(by, carry):
            copy_of(by).wait()
            return carry

        return (
            lambda: lax.fori_loop(1, sizes[axis], start, 0),
            lambda: lax.fori_loop(1, sizes[axis], wait, 0),
        )

    start_one, wait_one = exchange(1, energy_one, got_one, send_one, recv_one)
    start_two, wait_two = exchange(0, energy_two, got_two, send_two, recv_two)
    energy_one[...] = jnp.broadcast_to(jnp.sum(energy[...], axis=1, keepdims=True), energy_one.shape)
    start_one()

    def place_of(turn):
        return jnp.where(turn < 2 * n_cross, start_x + turn, turn - 2 * n_cross)

    def network(turn):
        step = place_of(turn)
        rows = keep_rows[step]
        hold_i[...], hold_j[...], hold_d[...] = backward(
            keep_down[step], keep_slope[step], rows[0:8], rows[8:16], rows[16:17], rows[17:18], w_hidden[...], wb[...],
            width,
        )

    def scatter(turn):
        step = place_of(turn)
        ids = keep_ids[step]
        acc_i[...] += scatter_product(hold_i[...], -hold_d[...], ids[0:1], spans)
        acc_j[side_of(step)] += scatter_product(hold_j[...], hold_d[...], ids[1:2], spans)

    network(0)

    def behind(turn, carry):
        scatter(turn - 1)
        network(turn)
        for axis in (0, 1):

            @pl.when(turn == (axis + 1) * n_cross)
            def _():
                message[axis] = acc_j[axis + 1].astype(BF16)
                returns[axis].start()

        @pl.when(turn == n_all // 2)
        def _():
            wait_one()
            energy_two[...] = energy_one[...] + jnp.sum(got_one[1:n_gy], axis=0)
            start_two()

        return carry

    lax.fori_loop(1, n_all, behind, 0)
    scatter(n_all - 1)
    for group in halos:
        for copy in group:
            copy.wait_send()
    for back in returns:
        back.wait()
    sums_out[...] = acc_i[...] + acc_j[0] + message_n[0].astype(F32) + message_n[1].astype(F32)
    wait_two()
    total = energy_two[...] + jnp.sum(got_two[1:n_gx], axis=0)
    energy_out[...] = total[0:1, 0:1] / (atoms * n_gx * n_gy)


def finish(energy_in, sums, energy, forces, feat):
    width, atoms = feat.shape
    spans = atoms // LO
    energy[...] = energy_in[...]
    for h in range(spans):
        cols = slice(h * LO, (h + 1) * LO)
        rows = slice(h * width, (h + 1) * width)
        feat[:, cols] = sums[rows, :]
        top = spans * width + 4 * h
        forces[:, cols] = -sums[top : top + 3, :]


def on_device(
    positions, features, halo_lists, local_pairs, cross_x, cross_y, pair_counts,
    w_rbf, w_src, w_dst, species_src, species_dst, w_hidden, w_latent, w_energy,
):
    width, atoms = features.shape
    hid = w_hidden.shape[0]
    n_gx, n_gy = lax.axis_size("gx"), lax.axis_size("gy")
    spans = atoms // LO
    rows = spans * width + spans * 4
    halo = halo_lists.shape[1]
    slots = local_pairs.shape[1] + cross_x.shape[1] + cross_y.shape[1]
    vmem = pl.BlockSpec(memory_space=pltpu.VMEM)
    dma = pltpu.SemaphoreType.DMA
    sums = jax.ShapeDtypeStruct((rows, LO), F32)
    one = jax.ShapeDtypeStruct((1, 1), F32)
    partial = pl.pallas_call(
        functools.partial(kernel, (n_gx, n_gy)),
        in_specs=[pl.BlockSpec(memory_space=pltpu.SMEM)] + [vmem] * 14,
        out_specs=[vmem] * 2,
        out_shape=[one, sums],
        scratch_shapes=[
            pltpu.VMEM((4, slots), jnp.int32),
            pltpu.VMEM((3, spans * width, LO), BF16),
            pltpu.VMEM((2, 8, halo), F32),
            pltpu.VMEM((2, 8, halo), F32),
            pltpu.VMEM((3, 8, atoms), F32),
            pltpu.VMEM((hid, 144), BF16),
            pltpu.VMEM((144, hid), BF16),
            pltpu.VMEM((hid, hid), BF16),
            pltpu.VMEM((hid, 128), F32),
            pltpu.VMEM((rows, LO), F32),
            pltpu.VMEM((3, rows, LO), F32),
            pltpu.VMEM((2, rows, LO), BF16),
            pltpu.VMEM((2, rows, LO), BF16),
            pltpu.VMEM((slots // BLK, hid, BLK), F32),
            pltpu.VMEM((slots // BLK, hid, BLK), BF16),
            pltpu.VMEM((slots // BLK, 24, BLK), F32),
            pltpu.VMEM((slots // BLK, 8, BLK), jnp.int32),
            pltpu.VMEM((width, BLK), F32),
            pltpu.VMEM((width, BLK), F32),
            pltpu.VMEM((8, BLK), F32),
            pltpu.VMEM((1, BLK), F32),
            pltpu.VMEM((1, 128), F32),
            pltpu.VMEM((1, 128), F32),
            pltpu.VMEM((n_gy, 1, 128), F32),
            pltpu.VMEM((n_gx, 1, 128), F32),
            dma((2, 3)),
            dma((2, 3)),
            dma((n_gy,)),
            dma((n_gy,)),
            dma((n_gx,)),
            dma((n_gx,)),
        ],
        compiler_params=pltpu.CompilerParams(
            collective_id=0, has_side_effects=True, vmem_limit_bytes=VMEM_LIMIT
        ),
        cost_estimate=pl.CostEstimate(flops=30000000000, bytes_accessed=4000000, transcendentals=0),
    )(
        pair_counts, local_pairs, cross_x, cross_y, positions, features, halo_lists,
        w_rbf, w_src, w_dst, species_src, species_dst, w_hidden, w_latent.T, w_energy.reshape(1, -1),
    )
    energy, forces, feat = pl.pallas_call(
        finish,
        in_specs=[vmem] * 2,
        out_specs=[vmem] * 3,
        out_shape=[
            one,
            jax.ShapeDtypeStruct((3, atoms), F32),
            jax.ShapeDtypeStruct((width, atoms), F32),
        ],
        compiler_params=pltpu.CompilerParams(vmem_limit_bytes=VMEM_LIMIT),
        cost_estimate=pl.CostEstimate(flops=1000000, bytes_accessed=2000000, transcendentals=0),
    )(*partial)
    return energy.reshape(1), forces, feat


def solution(mesh):
    split = P(None, ("gx", "gy"))
    return jax.shard_map(
        on_device,
        mesh=mesh,
        in_specs=(split,) * 6 + (P(("gx", "gy"), None),) + (P(),) * 8,
        out_specs=(P(), split, split),
        check_vma=False,
    )
```

```python
import functools
import math

import jax
import jax.numpy as jnp
from jax import lax
from jax.experimental import pallas as pl
from jax.experimental.pallas import tpu as pltpu
from jax.sharding import PartitionSpec as P

CUTOFF = 6.0
EDGE = 6.0
SOFT = 0.1
BLK = 2048
LO = 256
VMEM_LIMIT = 60 * 1024 * 1024
F32 = jnp.float32
BF16 = jnp.bfloat16
MESH = pl.DeviceIdType.MESH


def silu_parts(z):
    u = jnp.tanh(z) + 1.0
    y = z * u
    return y, u + y * (2.0 - u)


def sin_cos_pi(y):
    whole = jnp.floor(y + 0.5)
    t = (y - whole) * math.pi
    odd = whole - 2.0 * jnp.floor(whole * 0.5)
    sign = 1.0 - 2.0 * odd
    t2 = t * t
    s = -1.0 / 39916800.0
    for c in (1.0 / 362880.0, -1.0 / 5040.0, 1.0 / 120.0, -1.0 / 6.0, 1.0):
        s = s * t2 + c
    c_ = 1.0 / 479001600.0
    for c in (-1.0 / 3628800.0, 1.0 / 40320.0, -1.0 / 720.0, 1.0 / 24.0, -0.5, 1.0):
        c_ = c_ * t2 + c
    return s * t * sign, c_ * sign


def lane_lookup(table, index):
    parts = []
    for g in range(index.shape[1] // 128):
        ix = index[:, g * 128 : (g + 1) * 128]
        lane = ix & 127
        chunk = ix >> 7
        val = None
        for c in range(table.shape[1] // 128):
            got = jnp.take_along_axis(
                table[:, c * 128 : (c + 1) * 128], lane, axis=1, mode="promise_in_bounds"
            )
            val = got if c == 0 else jnp.where(chunk == c, got, val)
        parts.append(val)
    return jnp.concatenate(parts, axis=1)


def one_hot(index):
    low = (index & (LO - 1)).astype(F32).astype(BF16)
    rows = lax.broadcasted_iota(jnp.int32, (LO, index.shape[1]), 0).astype(F32).astype(BF16)
    return jnp.where(rows == low, jnp.ones((), BF16), jnp.zeros((), BF16))


def pick(table, index, width):
    got = jnp.dot(table, one_hot(index), preferred_element_type=F32)
    hi = index >> 8
    out = got[0:width]
    for h in range(1, table.shape[0] // width):
        out = jnp.where(hi == h, got[h * width : (h + 1) * width], out)
    return out


def scatter_product(feat, place, index, spans):
    hi = index >> 8
    half = lax.broadcasted_iota(jnp.int32, place.shape, 0) >> 2
    near = hi.astype(F32).astype(BF16)
    small = feat.astype(BF16)
    parts = [jnp.where(near == h, small, jnp.zeros((), BF16)) for h in range(spans)]
    pairs = [jnp.where(hi == 2 * g + half, place, 0.0) for g in range(spans // 2)]
    parts.append(jnp.concatenate(pairs, axis=0).astype(BF16))
    wide = jnp.concatenate(parts, axis=0)
    return lax.dot_general(
        wide, one_hot(index), (((1,), (1,)), ((), ())), preferred_element_type=F32
    )


def fill_weights(refs, wt, wb, wht, vec):
    w_rbf, w_src, w_dst, species_src, species_dst, w_hidden, w_latent_t, w_energy = refs
    stack = jnp.concatenate(
        [a[...].astype(F32) for a in (w_src, w_dst, w_rbf, species_src, species_dst)], axis=0
    )
    wb[...] = (stack * 0.25).astype(BF16)
    wt[...] = (stack * 0.5).T.astype(BF16)
    wht[...] = (w_hidden[...].astype(F32) * 0.5).T.astype(BF16)
    score = jnp.sum(w_latent_t[...].astype(F32).T * w_energy[...], axis=1, keepdims=True)
    vec[...] = jnp.broadcast_to(score, vec.shape)


def forward(first, second, kind_src, kind_dst, live, both, table_i, table_j, weights):
    wt, wht, vec = weights
    feats = table_i.shape[0] * LO // both.shape[1]
    ids = lax.broadcasted_iota(jnp.int32, (8, first.shape[1]), 0)
    found = lane_lookup(both, jnp.where(ids < 4, first, second))
    target = found[7:8].astype(jnp.int32)
    diff = jnp.where(ids < 3, jnp.concatenate([found[4:8], found[0:4]], axis=0) - found, 0.0)
    r = jnp.sqrt(jnp.sum(diff * diff, axis=0, keepdims=True) + SOFT)
    inv = 1.0 / r
    order = ids.astype(F32) + 1.0
    sine, cosine = sin_cos_pi(order * (r * (1.0 / CUTOFF)))
    basis = sine * inv
    slope = (order * (math.pi / CUTOFF) * cosine - basis) * inv
    species = jnp.where(ids == jnp.where(ids < 4, kind_src, kind_dst + 4), 1.0, 0.0)
    x = jnp.concatenate(
        [
            pick(table_i[...], first, feats).astype(BF16),
            pick(table_j[...], target, feats).astype(BF16),
            jnp.concatenate([basis, species], axis=0).astype(BF16),
        ],
        axis=0,
    )
    hidden, slope_one = silu_parts(jnp.dot(wt[...], x, preferred_element_type=F32))
    half = jnp.dot(wht[...], hidden.astype(BF16), preferred_element_type=F32)
    u = jnp.tanh(half) + 1.0
    scaled = u * vec[...][:, 0:1]
    top = half * scaled
    score = jnp.sum(top, axis=0, keepdims=True)
    down = (scaled + top * (2.0 - u)).astype(BF16)
    ratio = jnp.minimum(r * (1.0 / CUTOFF), 1.0)
    rest = 1.0 - ratio * ratio
    envelope = rest * rest * live
    by_cutoff = score * live * (rest * ratio * (-4.0 / CUTOFF))
    way = diff * inv
    way = way + jnp.concatenate([way[4:8], way[0:4]], axis=0)
    return envelope * score, slope_one, down, way, slope, envelope, by_cutoff, target


def backward(down, slope_one, way, slope, envelope, by_cutoff, w_hidden, wb, feats):
    back = jnp.dot(w_hidden, down, preferred_element_type=F32)
    grad_x = jnp.dot(wb, (back * slope_one).astype(BF16), preferred_element_type=F32) * envelope
    grad_r = jnp.sum(grad_x[2 * feats : 2 * feats + 8] * slope, axis=0, keepdims=True) + by_cutoff
    return grad_x[0:feats], grad_x[feats : 2 * feats], way * grad_r


def kernel(
    sizes, counts, local_pairs, pairs_x, pairs_y, positions, features, lists, w_rbf, w_src, w_dst, species_src,
    species_dst, w_hidden, w_latent, w_energy, energy_out, sums_out, pairs, tables, lent, lent_n, both, wt, wb,
    wht, vec, acc_i, acc_j, message, message_n, keep_slope, keep_down, keep_rows,
    keep_ids, hold_i, hold_j, hold_d, energy, energy_one, energy_two,
    got_one, got_two, send_sem, recv_sem, send_one, recv_one, send_two, recv_two,
):
    n_gx, n_gy = sizes
    gx, gy = lax.axis_index("gx"), lax.axis_index("gy")
    width, atoms = features.shape
    spans = atoms // LO
    halo = lists.shape[1]
    n_cross = pairs_x.shape[1] // BLK
    n_all = pairs.shape[1] // BLK
    start_x = local_pairs.shape[1] // BLK
    start_y = start_x + n_cross

    def peer(axis, by):
        if axis == 0:
            return (lax.rem(gx + by + n_gx, n_gx), gy)
        return (gx, lax.rem(gy + by + n_gy, n_gy))

    barrier = pltpu.get_barrier_semaphore()
    for axis in (0, 1):

        def greet(by, carry):
            pl.semaphore_signal(barrier, inc=1, device_id=peer(axis, by), device_id_type=MESH)
            return carry

        lax.fori_loop(1, sizes[axis], greet, 0)

    pairs[:, 0 : start_x * BLK] = local_pairs[...]
    pairs[:, start_x * BLK : start_y * BLK] = pairs_x[...]
    pairs[:, start_y * BLK :] = pairs_y[...]
    for h in range(spans):
        tables[0, h * width : (h + 1) * width, :] = features[:, h * LO : (h + 1) * LO]
    place = positions[...]
    zero = jnp.zeros((1, atoms), F32)
    number = lax.broadcasted_iota(jnp.int32, (1, atoms), 1).astype(F32)
    both[0] = jnp.concatenate([place, zero, place, number], axis=0)
    for axis in (0, 1):
        picked = lane_lookup(both[0], jnp.broadcast_to(lists[axis : axis + 1, :], (8, halo)))
        lent[axis] = picked
    fill_weights(
        (w_rbf, w_src, w_dst, species_src, species_dst, w_hidden, w_latent, w_energy), wt, wb, wht, vec
    )
    acc_i[...] = jnp.zeros_like(acc_i)
    acc_j[...] = jnp.zeros_like(acc_j)
    energy[...] = jnp.zeros_like(energy)

    def lend(axis, part, source, target, by):
        return pltpu.make_async_remote_copy(
            src_ref=source,
            dst_ref=target,
            send_sem=send_sem.at[axis, part],
            recv_sem=recv_sem.at[axis, part],
            device_id=peer(axis, by),
            device_id_type=MESH,
        )

    halos = [
        (
            lend(axis, 0, tables.at[0], tables.at[axis + 1], -1),
            lend(axis, 1, lent.at[axis], lent_n.at[axis], -1),
        )
        for axis in (0, 1)
    ]
    returns = [lend(axis, 2, message.at[axis], message_n.at[axis], 1) for axis in (0, 1)]

    def side_of(step):
        return jnp.where(step < start_x, 0, jnp.where(step < start_y, 1, 2))

    pl.semaphore_wait(barrier, n_gx + n_gy - 2)
    for group in halos:
        for copy in group:
            copy.start()

    def ahead(step, carry):
        for axis, begin in ((0, start_x), (1, start_y)):

            @pl.when(step == begin)
            def _():
                for copy in halos[axis]:
                    copy.wait_recv()
                ids = lax.broadcasted_iota(jnp.int32, (8, halo), 0)
                far = lent_n[axis] + jnp.where(ids == 4 + axis, EDGE, 0.0)
                both[axis + 1] = both[0]
                both[axis + 1, :, 0:halo] = jnp.where(ids < 4, both[0, :, 0:halo], far)

        side = side_of(step)
        skipped = jnp.where(side == 0, 0, jnp.where(side == 1, start_x, start_y))
        block = pairs[:, pl.ds(pl.multiple_of(step * BLK, BLK), BLK)]
        slot = (step - skipped) * BLK + lax.broadcasted_iota(jnp.int32, (1, BLK), 1)
        live = jnp.where(slot < counts[0, side], 1.0, 0.0)
        got = forward(
            block[0:1], block[1:2], block[2:3], block[3:4], live, both[side], tables.at[0], tables.at[side],
            (wt, wht, vec),
        )
        energy[...] += got[0]
        keep_slope[step] = got[1]
        keep_down[step] = got[2]
        keep_rows[step, 0:8] = got[3]
        keep_rows[step, 8:16] = got[4]
        keep_rows[step, 16:17] = got[5]
        keep_rows[step, 17:18] = got[6]
        keep_ids[step, 0:1] = block[0:1]
        keep_ids[step, 1:2] = got[7]
        return carry

    lax.fori_loop(0, n_all, ahead, 0)

    def exchange(axis, source, target, send, recv):
        def copy_of(by):
            return pltpu.make_async_remote_copy(
                src_ref=source,
                dst_ref=target.at[by],
                send_sem=send.at[by],
                recv_sem=recv.at[by],
                device_id=peer(axis, by),
                device_id_type=MESH,
            )

        def start(by, carry):
            copy_of(by).start()
            return carry

        def wait(by, carry):
            copy_of(by).wait()
            return carry

        return (
            lambda: lax.fori_loop(1, sizes[axis], start, 0),
            lambda: lax.fori_loop(1, sizes[axis], wait, 0),
        )

    start_one, wait_one = exchange(1, energy_one, got_one, send_one, recv_one)
    start_two, wait_two = exchange(0, energy_two, got_two, send_two, recv_two)
    energy_one[...] = jnp.broadcast_to(jnp.sum(energy[...], axis=1, keepdims=True), energy_one.shape)
    start_one()

    def place_of(turn):
        return jnp.where(turn < 2 * n_cross, start_x + turn, turn - 2 * n_cross)

    def network(turn):
        step = place_of(turn)
        rows = keep_rows[step]
        hold_i[...], hold_j[...], hold_d[...] = backward(
            keep_down[step], keep_slope[step], rows[0:8], rows[8:16], rows[16:17], rows[17:18], w_hidden[...], wb[...],
            width,
        )

    def scatter(turn):
        step = place_of(turn)
        ids = keep_ids[step]
        acc_i[...] += scatter_product(hold_i[...], -hold_d[...], ids[0:1], spans)
        acc_j[side_of(step)] += scatter_product(hold_j[...], hold_d[...], ids[1:2], spans)

    network(0)

    def behind(turn, carry):
        scatter(turn - 1)
        network(turn)
        for axis in (0, 1):

            @pl.when(turn == (axis + 1) * n_cross)
            def _():
                message[axis] = acc_j[axis + 1].astype(BF16)
                returns[axis].start()

        @pl.when(turn == n_all // 2)
        def _():
            wait_one()
            energy_two[...] = energy_one[...] + jnp.sum(got_one[1:n_gy], axis=0)
            start_two()

        return carry

    lax.fori_loop(1, n_all, behind, 0)
    scatter(n_all - 1)
    for group in halos:
        for copy in group:
            copy.wait_send()
    for back in returns:
        back.wait()
    sums_out[...] = acc_i[...] + acc_j[0] + message_n[0].astype(F32) + message_n[1].astype(F32)
    wait_two()
    total = energy_two[...] + jnp.sum(got_two[1:n_gx], axis=0)
    energy_out[...] = total[0:1, 0:1] / (atoms * n_gx * n_gy)


def finish(energy_in, sums, energy, forces, feat):
    width, atoms = feat.shape
    spans = atoms // LO
    energy[...] = energy_in[...]
    for h in range(spans):
        cols = slice(h * LO, (h + 1) * LO)
        rows = slice(h * width, (h + 1) * width)
        feat[:, cols] = sums[rows, :]
        top = spans * width + 4 * h
        forces[:, cols] = -sums[top : top + 3, :]


def on_device(
    positions, features, halo_lists, local_pairs, cross_x, cross_y, pair_counts,
    w_rbf, w_src, w_dst, species_src, species_dst, w_hidden, w_latent, w_energy,
):
    width, atoms = features.shape
    hid = w_hidden.shape[0]
    n_gx, n_gy = lax.axis_size("gx"), lax.axis_size("gy")
    spans = atoms // LO
    rows = spans * width + spans * 4
    halo = halo_lists.shape[1]
    slots = local_pairs.shape[1] + cross_x.shape[1] + cross_y.shape[1]
    vmem = pl.BlockSpec(memory_space=pltpu.VMEM)
    dma = pltpu.SemaphoreType.DMA
    sums = jax.ShapeDtypeStruct((rows, LO), F32)
    one = jax.ShapeDtypeStruct((1, 1), F32)
    partial = pl.pallas_call(
        functools.partial(kernel, (n_gx, n_gy)),
        in_specs=[pl.BlockSpec(memory_space=pltpu.SMEM)] + [vmem] * 14,
        out_specs=[vmem] * 2,
        out_shape=[one, sums],
        scratch_shapes=[
            pltpu.VMEM((4, slots), jnp.int32),
            pltpu.VMEM((3, spans * width, LO), BF16),
            pltpu.VMEM((2, 8, halo), F32),
            pltpu.VMEM((2, 8, halo), F32),
            pltpu.VMEM((3, 8, atoms), F32),
            pltpu.VMEM((hid, 144), BF16),
            pltpu.VMEM((144, hid), BF16),
            pltpu.VMEM((hid, hid), BF16),
            pltpu.VMEM((hid, 128), F32),
            pltpu.VMEM((rows, LO), F32),
            pltpu.VMEM((3, rows, LO), F32),
            pltpu.VMEM((2, rows, LO), BF16),
            pltpu.VMEM((2, rows, LO), BF16),
            pltpu.VMEM((slots // BLK, hid, BLK), F32),
            pltpu.VMEM((slots // BLK, hid, BLK), BF16),
            pltpu.VMEM((slots // BLK, 24, BLK), F32),
            pltpu.VMEM((slots // BLK, 8, BLK), jnp.int32),
            pltpu.VMEM((width, BLK), F32),
            pltpu.VMEM((width, BLK), F32),
            pltpu.VMEM((8, BLK), F32),
            pltpu.VMEM((1, BLK), F32),
            pltpu.VMEM((1, 128), F32),
            pltpu.VMEM((1, 128), F32),
            pltpu.VMEM((n_gy, 1, 128), F32),
            pltpu.VMEM((n_gx, 1, 128), F32),
            dma((2, 3)),
            dma((2, 3)),
            dma((n_gy,)),
            dma((n_gy,)),
            dma((n_gx,)),
            dma((n_gx,)),
        ],
        compiler_params=pltpu.CompilerParams(
            collective_id=0, has_side_effects=True, vmem_limit_bytes=VMEM_LIMIT
        ),
        cost_estimate=pl.CostEstimate(flops=30000000000, bytes_accessed=4000000, transcendentals=0),
    )(
        pair_counts, local_pairs, cross_x, cross_y, positions, features, halo_lists,
        w_rbf, w_src, w_dst, species_src, species_dst, w_hidden, w_latent.T, w_energy.reshape(1, -1),
    )
    energy, forces, feat = pl.pallas_call(
        finish,
        in_specs=[vmem] * 2,
        out_specs=[vmem] * 3,
        out_shape=[
            one,
            jax.ShapeDtypeStruct((3, atoms), F32),
            jax.ShapeDtypeStruct((width, atoms), F32),
        ],
        compiler_params=pltpu.CompilerParams(vmem_limit_bytes=VMEM_LIMIT),
        cost_estimate=pl.CostEstimate(flops=1000000, bytes_accessed=2000000, transcendentals=0),
    )(*partial)
    return energy.reshape(1), forces, feat


def solution(mesh):
    split = P(None, ("gx", "gy"))
    return jax.shard_map(
        on_device,
        mesh=mesh,
        in_specs=(split,) * 6 + (P(("gx", "gy"), None),) + (P(),) * 8,
        out_specs=(P(), split, split),
        check_vma=False,
    )
```
